256 devices in a mesh: dp: 8 (over x, core), vocab: 32 (over z, y).
Axes of the slice: x: 4, y: 4, z: 8, core: 2. Of those that a mesh axis runs over, the one named last changes fastest.
Arguments:
- hidden: bfloat16 [1024, 3584], P('dp'), may hold values from -64 to 64
- head_weight: bfloat16 [3584, 131072], P('dp', 'vocab'), may hold values from -0.15039062 to 0.15039062
- teacher_logits: float32 [1024, 131072], P('dp', 'vocab'), may hold values from -32 to 480
Outputs:
- divergence: float32 [1024], P('dp')
- hidden_gradient: bfloat16 [1024, 3584], P('vocab', 'dp')
- head_gradient: bfloat16 [3584, 131072], P('dp', 'vocab')
The draws below stay inside these ranges and needn't reach their ends.
All inputs are finite; a program needn't handle non-finite values.
Results may differ from the reference program's by a relative error of at most 0.0043.
Values may be sent and summed in bfloat16 or wider, within the bound.
A program may use at most 128 MiB of HBM per device.

```python
import math
import jax
import jax.numpy as jnp
from jax import lax

D = 3584
VOCAB = 131072
ROWS = 1024


def column_scales(key):
    scale_key = jax.random.fold_in(key, 11)
    return jnp.exp(jax.random.uniform(scale_key, (VOCAB,), jnp.float32, math.log(0.5), math.log(2.0)))


def head_base(key):
    normal_key = jax.random.fold_in(key, 12)
    values = jnp.clip(jax.random.normal(normal_key, (D, VOCAB), jnp.float32), -4.0, 4.0)
    return values * column_scales(key)[None, :] / math.sqrt(D)


def draw_head_weight(key, part):
    base = head_base(key)
    return jnp.clip(base, -0.15, 0.15).astype(jnp.bfloat16)


def draw_hidden(key, part):
    key = jax.random.fold_in(key, 2)
    normal_key, scale_key = jax.random.split(key, 2)
    row_scale = jnp.exp(jax.random.uniform(scale_key, (ROWS, 1), jnp.float32, 0.0, math.log(8.0)))
    values = jnp.clip(jax.random.normal(normal_key, (ROWS, D), jnp.float32), -4.0, 4.0) * row_scale
    return jnp.clip(values, -64.0, 64.0).astype(jnp.bfloat16)


def draw_teacher_logits(key, part):
    key = jax.random.fold_in(key, 3)
    normal_key, scale_key = jax.random.split(key, 2)
    row_scale = jnp.exp(jax.random.uniform(scale_key, (ROWS, 1), jnp.float32, 0.0, math.log(8.0)))
    values = jnp.clip(jax.random.normal(normal_key, (ROWS, VOCAB), jnp.float32), -4.0, 4.0) * row_scale
    return jnp.clip(values, -32.0, 480.0)


def setup_inputs(seed: int = 0) -> dict:
    arg_keys = jax.random.split(jax.random.key(seed), 4)
    return {
        "hidden": draw_hidden(jax.random.fold_in(arg_keys[3], 71), 0),
        "head_weight": draw_head_weight(jax.random.fold_in(arg_keys[3], 71), 0),
        "teacher_logits": draw_teacher_logits(jax.random.fold_in(arg_keys[3], 71), 0),
    }


loss_scale = 256.0


def reference(hidden, head_weight, teacher_logits):
    student = jnp.dot(hidden, head_weight, preferred_element_type=jnp.float32)
    student_max = jnp.max(student, axis=1)
    teacher_max = jnp.max(teacher_logits, axis=1)
    student_exp = jnp.exp(student - student_max[:, None])
    teacher_exp = jnp.exp(teacher_logits - teacher_max[:, None])
    student_sum = jnp.sum(student_exp, axis=1)
    teacher_sum = jnp.sum(teacher_exp, axis=1)
    cross_sum = jnp.sum(teacher_exp * (teacher_logits - student), axis=1)
    divergence = cross_sum / teacher_sum - teacher_max - jnp.log(teacher_sum) + student_max + jnp.log(student_sum)
    grad_logits = (loss_scale * (student_exp / student_sum[:, None] - teacher_exp / teacher_sum[:, None])).astype(jnp.bfloat16)
    hidden_gradient = lax.dot_general(grad_logits, head_weight, (((1,), (1,)), ((), ())), preferred_element_type=jnp.float32).astype(jnp.bfloat16)
    head_gradient = lax.dot_general(hidden, grad_logits, (((0,), (0,)), ((), ())), preferred_element_type=jnp.float32).astype(jnp.bfloat16)
    return divergence, hidden_gradient, head_gradient
```

```python
import jax
import jax.numpy as jnp
from jax import lax
from jax.experimental import pallas as pl
from jax.experimental.pallas import tpu as pltpu
from jax.sharding import PartitionSpec as P

MESH = pl.DeviceIdType.MESH
F32, BF16 = jnp.float32, jnp.bfloat16
loss_scale = 256.0
LOW = -3.0e38

D, ROWS = 3584, 1024
NX, NY, NZ = 4, 4, 8
BLK = 128
SUB = BLK // NY
WID = D // 8
CHIP = 2 * WID
COLS = 4096
PART = COLS // NX
HSH = D // NY


def groups(value):
    return [value[:, 128 * g : 128 * g + 128] for g in range(value.shape[1] // 128)]


def fold(parts, op):
    while len(parts) > 1:
        parts = [op(parts[i], parts[i + 1]) for i in range(0, len(parts), 2)]
    return parts[0]


def row_max(part):
    return jnp.max(part.T, axis=0, keepdims=True)


def row_sum(part):
    return jnp.sum(part.T, axis=0, keepdims=True)


def kernel(
    h_ref, w_ref, t_ref,
    div_ref, hg_ref, dw_ref,
    hc, wc, tc, student, town, wown, wt, hx, ht, gbuf, acc, stage,
    hgp, hgy, hgz, sx, sy, sz, col, cross, cx, cy, cz,
    lsem, osem, hxs, hxr, hys, hyr, wxs, wxr, wcs, wcr, ts, tr, hcs, hcr,
    sxs, sxr, sys_, syr, szs, szr, gas, gar, gfs, gfr, gcs, gcr,
    hgys, hgyr, hgzs, hgzr, cxs, cxr, cys, cyr, czs, czr,
):
    dp, v = lax.axis_index("dp"), lax.axis_index("vocab")
    x, c = dp // 2, dp % 2
    z, y = v // NY, v % NY

    def at_x(o):
        return (lax.rem(x + o, NX) * 2 + c, v)

    def at_y(o):
        return (dp, z * NY + lax.rem(y + o, NY))

    def at_z(o):
        return (dp, lax.rem(z + o, NZ) * NY + y)

    other = (x * 2 + 1 - c, v)

    def remote(src, dst, ss, rs, device):
        return pltpu.make_async_remote_copy(
            src_ref=src, dst_ref=dst, send_sem=ss, recv_sem=rs, device_id=device, device_id_type=MESH
        )

    barrier = pltpu.get_barrier_semaphore()
    partners = [at_x(o) for o in range(1, NX)] + [other]
    partners += [at_y(o) for o in range(1, NY)] + [at_z(o) for o in range(1, NZ)]
    for p in partners:
        pl.semaphore_signal(barrier, inc=1, device_id=p, device_id_type=MESH)

    def cols_of(i):
        return pl.ds(pl.multiple_of(i * PART, PART), PART)

    def rows_of(i):
        return pl.ds(pl.multiple_of(i * BLK, BLK), BLK)

    def wrows(i, j):
        return pl.ds(pl.multiple_of(i * CHIP + j * WID, 64), WID)

    own_w = pltpu.make_async_copy(w_ref.at[:, cols_of(x)], wc.at[wrows(x, c)], lsem.at[0])
    share = pl.ds(pl.multiple_of(y * HSH, HSH), HSH)
    own_h = pltpu.make_async_copy(h_ref.at[:, share], hc.at[rows_of(x), share], lsem.at[1])
    own_t = pltpu.make_async_copy(t_ref.at[:, cols_of(x)], tc.at[x], lsem.at[2])
    all_t = pltpu.make_async_copy(t_ref, town, lsem.at[3])
    all_w = pltpu.make_async_copy(w_ref, wown, lsem.at[4])
    for cp in (own_h, all_t, all_w, own_w, own_t):
        cp.start()
    pl.semaphore_wait(barrier, len(partners))

    h_x = [
        remote(h_ref.at[:, share], hc.at[rows_of(x), share], hxs.at[o - 1], hxr.at[o - 1], at_x(o))
        for o in range(1, NX)
    ]
    w_x = [
        remote(
            w_ref.at[:, cols_of(lax.rem(x + o, NX))], wc.at[wrows(x, c)], wxs.at[o - 1], wxr.at[o - 1], at_x(o)
        )
        for o in range(1, NX)
    ]
    t_x = [
        remote(t_ref.at[:, cols_of(lax.rem(x + o, NX))], tc.at[x], ts.at[o - 1], tr.at[o - 1], at_x(o))
        for o in range(1, NX)
    ]

    def w_core(o):
        rows = wrows(lax.rem(x + NX - o, NX), c)
        src = w_ref.at[:, cols_of(x)] if o == 0 else wc.at[rows]
        return remote(src, wc.at[rows], wcs.at[o], wcr.at[o], other)

    w_c = [w_core(o) for o in range(NX)]
    for cp in h_x + w_x:
        cp.start()
    w_c[0].start()

    own_h.wait()
    for cp in h_x:
        cp.wait_recv()
    h_y = [
        remote(hc.at[:, share], hc.at[:, share], hys.at[o - 1], hyr.at[o - 1], at_y(o)) for o in range(1, NY)
    ]
    for cp in h_y:
        cp.start()

    for b in range(NX):
        sx[x, b] = jnp.where(lax.broadcasted_iota(jnp.int32, (8, BLK), 0) % 2 == 0, LOW, 0.0)
    all_t.wait()
    part = fold([town[:, 128 * g : 128 * g + 128] for g in range(COLS // 128)], jnp.maximum)
    top = jnp.max(part, axis=1, keepdims=True)
    total = fold([jnp.exp(town[:, 128 * g : 128 * g + 128] - top) for g in range(COLS // 128)], jnp.add)
    sx[x, x, 2:3, :] = row_max(part)
    sx[x, x, 3:4, :] = row_sum(total)

    all_w.wait()

    def turn(i, carry):
        cols = pl.ds(pl.multiple_of(i * 512, 512), 512)
        wt[cols, :] = wown[:, cols].T
        return carry

    lax.fori_loop(0, COLS // 512, turn, 0)

    for o in (1, 3, 2):
        w_x[o - 1].wait_recv()
        w_c[o].start()
    for cp in w_x:
        cp.wait_send()
    for cp in t_x:
        cp.start()
    for cp in h_y:
        cp.wait_recv()

    mine = pl.ds(pl.multiple_of(x * CHIP, CHIP), CHIP)
    h_c = remote(hc.at[:, mine], hx.at[c], hcs.at[0], hcr.at[0], other)
    h_c.start()
    keep = pltpu.make_async_copy(hc.at[:, mine], hx.at[c], lsem.at[5])
    keep.start()
    own_w.wait()
    for cp in w_c:
        cp.wait_recv()

    def score(i, carry):
        cols = pl.ds(pl.multiple_of(i * 256, 256), 256)
        tile = jnp.dot(hc[...], wc[:, cols], preferred_element_type=F32)
        student[:, :, cols] = tile.reshape(NX, BLK, 256)
        return carry

    lax.fori_loop(0, PART // 256, score, 0)

    def local_stats(b, carry):
        parts = groups(student[b])
        part = fold(parts, jnp.maximum)
        top = jnp.max(part, axis=1, keepdims=True)
        total = fold([jnp.exp(p - top) for p in parts], jnp.add)
        sx[x, b, 0:1, :] = row_max(part)
        sx[x, b, 1:2, :] = row_sum(total)
        return carry

    lax.fori_loop(0, NX, local_stats, 0)

    def reduce_stats(slots, count, target):
        for b in range(NX):
            m_s = fold([slots[i, b, 0:1, :] for i in range(count)], jnp.maximum)
            m_t = fold([slots[i, b, 2:3, :] for i in range(count)], jnp.maximum)
            l_s = fold([slots[i, b, 1:2, :] * jnp.exp(slots[i, b, 0:1, :] - m_s) for i in range(count)], jnp.add)
            l_t = fold([slots[i, b, 3:4, :] * jnp.exp(slots[i, b, 2:3, :] - m_t) for i in range(count)], jnp.add)
            target(b, m_s, l_s, m_t, l_t)

    def into(slots, me):
        def put(b, *values):
            for r, value in enumerate(values):
                slots[me, b, r : r + 1, :] = value

        return put

    s_x = [remote(sx.at[x], sx.at[x], sxs.at[o - 1], sxr.at[o - 1], at_x(o)) for o in range(1, NX)]
    s_y = [remote(sy.at[y], sy.at[y], sys_.at[o - 1], syr.at[o - 1], at_y(o)) for o in range(1, NY)]
    s_z = [remote(sz.at[z], sz.at[z], szs.at[o - 1], szr.at[o - 1], at_z(o)) for o in range(1, NZ)]
    for cp in s_x:
        cp.start()
    keep.wait()
    h_c.wait_recv()

    def turn_h(k, carry):
        rows = [
            hx[j, pl.ds(pl.multiple_of(BLK * b + SUB * k, SUB), SUB), :] for j in range(2) for b in range(NX)
        ]
        block = jnp.concatenate(rows, axis=0).astype(F32)
        block = pltpu.roll(block, lax.rem(c * WID, CHIP), 1)[:, :512]
        ht[k] = block.T[:WID].astype(BF16)
        return carry

    lax.fori_loop(0, NY, turn_h, 0)
    for cp in s_x:
        cp.wait_recv()
    reduce_stats(sx, NX, into(sy, y))
    for cp in s_y:
        cp.start()
    for cp in s_y:
        cp.wait_recv()
    reduce_stats(sy, NY, into(sz, z))
    for cp in s_z:
        cp.start()
    for cp in s_z:
        cp.wait_recv()

    def columns(b, m_s, l_s, m_t, l_t):
        for r, value in enumerate((m_s, loss_scale / l_s, m_t, loss_scale / l_t)):
            col[r, b] = jnp.broadcast_to(value, (BLK, BLK)).T
        sx[0, b, 4:5, :] = m_s + jnp.log(l_s) - m_t - jnp.log(l_t)
        sx[0, b, 5:6, :] = l_t

    for cp in s_x:
        cp.wait_send()
    reduce_stats(sz, NZ, columns)

    own_t.wait()
    for cp in t_x:
        cp.wait_recv()

    def half(s, owner, first):
        return gbuf.at[s, pl.ds(pl.multiple_of(c * BLK + first, 64), BLK // 2), cols_of(owner)]

    def whole(s, owner):
        return gbuf.at[s, pl.ds(pl.multiple_of(c * BLK, BLK), BLK), cols_of(owner)]

    left, right, far = lax.rem(x + 3, NX), lax.rem(x + 1, NX), lax.rem(x + 2, NX)
    owners = [x, left, far, right]
    g_a, g_f, g_c = [], [], []
    for s in range(NY):
        g_a.append(
            [remote(whole(s, x), whole(s, x), gas.at[s, i], gar.at[s, i], at_x(o)) for i, o in enumerate((1, 3))]
        )
        g_f.append(
            [
                remote(half(s, left, 0), half(s, left, 0), gfs.at[s, 0], gfr.at[s, 0], at_x(1)),
                remote(half(s, right, 64), half(s, right, 64), gfs.at[s, 1], gfr.at[s, 1], at_x(3)),
            ]
        )
        g_c.append(
            [remote(whole(s, q), whole(s, q), gcs.at[s, o], gcr.at[s, o], other) for o, q in enumerate(owners)]
        )

    for s in range(NY):
        k = lax.rem(y + 1 + s, NY)
        rows = pl.ds(pl.multiple_of(k * SUB, SUB), SUB)

        def grad(b, carry):
            m_s, a_s, m_t, a_t = [col[r, b, rows, :] for r in range(4)]
            out = pl.ds(pl.multiple_of(c * BLK + b * SUB, SUB), SUB)
            total = jnp.zeros((SUB, 128), F32)
            tiles = []
            for g in range(PART // 128):
                st = student[b, rows, 128 * g : 128 * g + 128]
                te = tc[b, rows, 128 * g : 128 * g + 128]
                e_t = jnp.exp(te - m_t)
                total += e_t * (te - st)
                tiles.append((jnp.exp(st - m_s) * a_s - e_t * a_t).astype(BF16))
            gbuf[s, out, cols_of(x)] = jnp.concatenate(tiles, axis=1)
            cross[b, rows, :] = total
            return carry

        lax.fori_loop(0, NX, grad, 0)
        for cp in g_a[s]:
            cp.start()
        g_c[s][0].start()

    for b in range(NX):
        cx[x, b] = jnp.broadcast_to(row_sum(cross[b]), (8, BLK))
    c_x = [
        remote(
            cx.at[x, lax.rem(x + o, NX)], cx.at[x, lax.rem(x + o, NX)], cxs.at[o - 1], cxr.at[o - 1], at_x(o)
        )
        for o in range(1, NX)
    ]
    c_y = [remote(cy.at[y], cy.at[y], cys.at[o - 1], cyr.at[o - 1], at_y(o)) for o in range(1, NY)]
    c_z = [remote(cz.at[z], cz.at[z], czs.at[o - 1], czr.at[o - 1], at_z(o)) for o in range(1, NZ)]
    for cp in c_x:
        cp.start()

    h_to_y = [
        remote(hgp.at[o - 1], hgy.at[o - 1], hgys.at[o - 1], hgyr.at[o - 1], at_y(o)) for o in range(1, NY)
    ]

    def z_rows(o):
        zz = lax.rem(z + o, NZ)
        return pl.ds(pl.multiple_of((zz % 2) * BLK + (zz // 2) * SUB, SUB), SUB)

    h_to_z = [
        remote(hgp.at[3, z_rows(o)], hgz.at[o - 1], hgzs.at[o - 1], hgzr.at[o - 1], at_z(o))
        for o in range(1, NZ)
    ]
    d_out = []
    for s in range(NY):
        k = lax.rem(y + 1 + s, NY)
        g_a[s][0].wait_recv()
        g_f[s][0].start()
        g_c[s][1].start()
        g_a[s][1].wait_recv()
        g_f[s][1].start()
        g_c[s][3].start()
        for cp in g_f[s]:
            cp.wait_recv()
        g_c[s][2].start()
        if s == 1:
            for cp in c_x:
                cp.wait_recv()
            cy[y] = cx[0, x] + cx[1, x] + cx[2, x] + cx[3, x]
            for cp in c_y:
                cp.start()
        if s == 2:
            for cp in c_y:
                cp.wait_recv()
            cz[z] = cy[0] + cy[1] + cy[2] + cy[3]
            for cp in c_z:
                cp.start()
        for cp in g_c[s]:
            cp.wait_recv()
        product = jnp.dot(gbuf[s], wt[...], preferred_element_type=F32)
        if s < 3:
            hgp[s] = product
            h_to_y[s].start()
        else:
            for cp in h_to_y:
                cp.wait_recv()
            hgp[3] = product + hgy[0] + hgy[1] + hgy[2]
            for cp in h_to_z:
                cp.start()

        def head(i, carry):
            cols = pl.ds(pl.multiple_of(i * 512, 512), 512)
            tile = jnp.dot(ht[k], gbuf[s, :, cols], preferred_element_type=F32)
            if s == 0:
                acc[:, cols] = tile
            elif s < 3:
                acc[:, cols] += tile
            else:
                stage[:, cols] = (acc[:, cols] + tile).astype(BF16)
            return carry

        if s < 3:
            lax.fori_loop(0, COLS // 512, head, 0)
        else:
            for i in range(NX):
                lax.fori_loop(2 * i, 2 * i + 2, head, 0)
                cols = pl.ds(i * PART, PART)
                d_out.append(pltpu.make_async_copy(stage.at[:, cols], dw_ref.at[:, cols], osem.at[i]))
                d_out[-1].start()

    for cp in c_z:
        cp.wait_recv()
    crossed = fold([cz[i, 0:1, :] for i in range(NZ)], jnp.add)
    div_ref[...] = crossed / sx[0, x, 5:6, :] + sx[0, x, 4:5, :]

    for cp in h_to_z:
        cp.wait_recv()
    total = hgp[3, z_rows(0), :]
    for i in range(NZ - 1):
        total = total + hgz[i]
    hg_ref[...] = total.astype(BF16)

    for cp in d_out:
        cp.wait()
    sent = h_x + w_c + h_y + t_x + [h_c] + s_y + s_z + c_x + c_y + c_z + h_to_y + h_to_z
    for cp in sent + sum(g_a, []) + sum(g_f, []) + sum(g_c, []):
        cp.wait_send()


def local(hidden, head_weight, teacher_logits):
    dma = pltpu.SemaphoreType.DMA
    vmem = pltpu.VMEM
    scratch = [
        vmem((NX * BLK, D), BF16),
        vmem((D, PART), BF16),
        vmem((NX, BLK, PART), F32),
        vmem((NX, BLK, PART), F32),
        vmem((BLK, COLS), F32),
        vmem((WID, COLS), BF16),
        vmem((COLS, WID), BF16),
        vmem((2, NX * BLK, CHIP), BF16),
        vmem((NY, WID, 2 * BLK), BF16),
        vmem((NY, 2 * BLK, COLS), BF16),
        vmem((WID, COLS), F32),
        vmem((WID, COLS), BF16),
        vmem((NY, 2 * BLK, WID), F32),
        vmem((NY - 1, 2 * BLK, WID), F32),
        vmem((NZ - 1, SUB, WID), F32),
        vmem((NX, NX, 8, BLK), F32),
        vmem((NY, NX, 8, BLK), F32),
        vmem((NZ, NX, 8, BLK), F32),
        vmem((4, NX, BLK, BLK), F32),
        vmem((NX, BLK, BLK), F32),
        vmem((NX, NX, 8, BLK), F32),
        vmem((NY, 8, BLK), F32),
        vmem((NZ, 8, BLK), F32),
    ]
    counts = [(3,), (3,), (3,), (4,), (3,), (1,), (3,), (3,), (7,), (4, 2), (4, 2), (4, 4), (3,), (7,), (3,), (3,), (7,)]
    sems = [dma((6,)), dma((4,))]
    for n in counts:
        sems += [dma(n), dma(n)]
    div, hg, dw = pl.pallas_call(
        kernel,
        name="distill",
        out_shape=(
            jax.ShapeDtypeStruct((1, BLK), F32),
            jax.ShapeDtypeStruct((SUB, WID), BF16),
            jax.ShapeDtypeStruct((WID, COLS), BF16),
        ),
        in_specs=[pl.BlockSpec(memory_space=pl.ANY)] * 3,
        out_specs=(
            pl.BlockSpec(memory_space=pltpu.VMEM),
            pl.BlockSpec(memory_space=pltpu.VMEM),
            pl.BlockSpec(memory_space=pl.ANY),
        ),
        scratch_shapes=scratch + sems,
        compiler_params=pltpu.CompilerParams(
            collective_id=0, has_side_effects=True, vmem_limit_bytes=60 * 1024 * 1024
        ),
    )(hidden, head_weight, teacher_logits)
    return div.reshape(BLK), hg, dw


def solution(mesh):
    return jax.shard_map(
        local,
        mesh=mesh,
        in_specs=(P("dp", None), P("dp", "vocab"), P("dp", "vocab")),
        out_specs=(P("dp"), P("vocab", "dp"), P("dp", "vocab")),
        check_vma=False,
    )
```

```python
import jax
import jax.numpy as jnp
from jax import lax
from jax.experimental import pallas as pl
from jax.experimental.pallas import tpu as pltpu
from jax.sharding import PartitionSpec as P

MESH = pl.DeviceIdType.MESH
F32, BF16 = jnp.float32, jnp.bfloat16
loss_scale = 256.0
LOW = -3.0e38

D, ROWS = 3584, 1024
NX, NY, NZ = 4, 4, 8
BLK = 128
SUB = BLK // NY
WID = D // 8
CHIP = 2 * WID
COLS = 4096
PART = COLS // NX
HSH = D // NY
HALF = BLK // 2


STEPS = ((1, 0, 32), (2, 0, 32), (3, 0, 32), (0, 0, 16), (0, 16, 16))
BIG = 2 * NX * SUB
FIRST = (0, BIG, 2 * BIG, 3 * BIG, 3 * BIG + BIG // 2)


def groups(value):
    return [value[:, 128 * g : 128 * g + 128] for g in range(value.shape[1] // 128)]


def fold(parts, op):
    while len(parts) > 1:
        parts = [op(parts[i], parts[i + 1]) for i in range(0, len(parts), 2)]
    return parts[0]


def row_max(part):
    return jnp.max(part.T, axis=0, keepdims=True)


def row_sum(part):
    return jnp.sum(part.T, axis=0, keepdims=True)


def kernel(
    h_ref, w_ref, t_ref,
    div_ref, hg_ref, dw_ref,
    hc, wc, tc, student, town, wown, wt, hx, ht, gbuf, acc,
    hgp, hgy, hgz, sx, sy, sz, last, col, cross, cx, cy, cz,
    lsem, hxs, hxr, hzs, hzr, hys, hyr, wxs, wxr, wcs, wcr, ts, tr, hcs, hcr,
    sxs, sxr, sys_, syr, szs, szr, gas, gar, gfs, gfr, gcs, gcr,
    hgys, hgyr, hgzs, hgzr, cxs, cxr, cys, cyr, czs, czr,
):
    dp, v = lax.axis_index("dp"), lax.axis_index("vocab")
    x, c = dp // 2, dp % 2
    z, y = v // NY, v % NY

    def at_x(o):
        return (lax.rem(x + o, NX) * 2 + c, v)

    def at_y(o):
        return (dp, z * NY + lax.rem(y + o, NY))

    def at_z(o):
        return (dp, lax.rem(z + o, NZ) * NY + y)

    other = (x * 2 + 1 - c, v)
    beside = (dp, (z + 1 - 2 * (z % 2)) * NY + y)

    def remote(src, dst, ss, rs, device):
        return pltpu.make_async_remote_copy(
            src_ref=src, dst_ref=dst, send_sem=ss, recv_sem=rs, device_id=device, device_id_type=MESH
        )

    barrier = pltpu.get_barrier_semaphore()
    partners = [at_x(o) for o in range(1, NX)] + [other]
    partners += [at_y(o) for o in range(1, NY)] + [at_z(o) for o in range(1, NZ)]
    for p in partners:
        pl.semaphore_signal(barrier, inc=1, device_id=p, device_id_type=MESH)

    def cols_of(i):
        return pl.ds(pl.multiple_of(i * PART, PART), PART)

    def wrows(i, j):
        return pl.ds(pl.multiple_of(i * CHIP + j * WID, 64), WID)

    own_w = pltpu.make_async_copy(w_ref.at[:, cols_of(x)], wc.at[wrows(x, c)], lsem.at[0])
    share = pl.ds(pl.multiple_of(y * HSH, HSH), HSH)
    half_of = [pl.ds(pl.multiple_of((z % 2) * HALF, HALF), HALF), pl.ds(pl.multiple_of((1 - z % 2) * HALF, HALF), HALF)]
    own_h = pltpu.make_async_copy(h_ref.at[half_of[0], share], hc.at[x, half_of[0], share], lsem.at[1])
    own_t = pltpu.make_async_copy(t_ref.at[:, cols_of(x)], tc.at[x], lsem.at[2])
    all_t = pltpu.make_async_copy(t_ref, town, lsem.at[3])
    all_w = pltpu.make_async_copy(w_ref, wown, lsem.at[4])
    for cp in (own_h, all_t, all_w, own_w, own_t):
        cp.start()
    pl.semaphore_wait(barrier, len(partners))

    h_x = [
        remote(
            h_ref.at[half_of[0], share], hc.at[x, half_of[0], share], hxs.at[o - 1], hxr.at[o - 1], at_x(o)
        )
        for o in range(1, NX)
    ]
    w_x = [
        remote(
            w_ref.at[:, cols_of(lax.rem(x + o, NX))], wc.at[wrows(x, c)], wxs.at[o - 1], wxr.at[o - 1], at_x(o)
        )
        for o in range(1, NX)
    ]
    t_x = [
        remote(t_ref.at[:, cols_of(lax.rem(x + o, NX))], tc.at[x], ts.at[o - 1], tr.at[o - 1], at_x(o))
        for o in range(1, NX)
    ]

    def w_core(o):
        rows = wrows(lax.rem(x + NX - o, NX), c)
        src = w_ref.at[:, cols_of(x)] if o == 0 else wc.at[rows]
        return remote(src, wc.at[rows], wcs.at[o], wcr.at[o], other)

    w_c = [w_core(o) for o in range(NX)]
    for cp in h_x + w_x:
        cp.start()
    w_c[0].start()

    own_h.wait()
    for cp in h_x:
        cp.wait_recv()
    shares = [hc.at[:, rows, share] for rows in half_of]
    h_z = remote(shares[0], shares[0], hzs.at[0], hzr.at[0], beside)
    h_y = [
        [remote(part, part, hys.at[i, o - 1], hyr.at[i, o - 1], at_y(o)) for o in range(1, NY)]
        for i, part in enumerate(shares)
    ]
    h_z.start()
    for cp in h_y[0]:
        cp.start()

    for b in range(NX):
        sy[y, b] = jnp.where(lax.broadcasted_iota(jnp.int32, (8, BLK), 0) % 2 == 0, LOW, 0.0)
    all_t.wait()
    part = fold([town[:, 128 * g : 128 * g + 128] for g in range(COLS // 128)], jnp.maximum)
    top = jnp.max(part, axis=1, keepdims=True)
    total = fold([jnp.exp(town[:, 128 * g : 128 * g + 128] - top) for g in range(COLS // 128)], jnp.add)
    sy[y, x, 2:3, :] = row_max(part)
    sy[y, x, 3:4, :] = row_sum(total)

    all_w.wait()

    def turn(i, carry):
        cols = pl.ds(pl.multiple_of(i * 512, 512), 512)
        wt[cols, :] = wown[:, cols].T
        return carry

    lax.fori_loop(0, COLS // 512, turn, 0)

    h_z.wait_recv()
    for cp in h_y[1]:
        cp.start()
    for o in (1, 3, 2):
        w_x[o - 1].wait_recv()
        w_c[o].start()
    for cp in w_x:
        cp.wait_send()
    for cp in t_x:
        cp.start()
    for cp in h_y[0] + h_y[1]:
        cp.wait_recv()

    mine = pl.ds(pl.multiple_of(x * CHIP, CHIP), CHIP)
    h_c = remote(hc.at[:, :, mine], hx.at[c], hcs.at[0], hcr.at[0], other)
    h_c.start()
    keep = pltpu.make_async_copy(hc.at[:, :, mine], hx.at[c], lsem.at[5])
    keep.start()
    own_w.wait()
    for cp in w_c:
        cp.wait_recv()

    def score(i, carry):
        cols = pl.ds(pl.multiple_of(i * 256, 256), 256)
        tile = jnp.dot(hc[...].reshape(NX * BLK, D), wc[:, cols], preferred_element_type=F32)
        student[:, :, cols] = tile.reshape(NX, BLK, 256)
        return carry

    lax.fori_loop(0, PART // 256, score, 0)

    def local_stats(b, carry):
        parts = groups(student[b])
        part = fold(parts, jnp.maximum)
        top = jnp.max(part, axis=1, keepdims=True)
        total = fold([jnp.exp(p - top) for p in parts], jnp.add)
        sy[y, b, 0:1, :] = row_max(part)
        sy[y, b, 1:2, :] = row_sum(total)
        return carry

    lax.fori_loop(0, NX, local_stats, 0)

    def reduce_stats(slots, count, target):
        for b in range(NX):
            m_s = fold([slots[i, b, 0:1, :] for i in range(count)], jnp.maximum)
            m_t = fold([slots[i, b, 2:3, :] for i in range(count)], jnp.maximum)
            l_s = fold([slots[i, b, 1:2, :] * jnp.exp(slots[i, b, 0:1, :] - m_s) for i in range(count)], jnp.add)
            l_t = fold([slots[i, b, 3:4, :] * jnp.exp(slots[i, b, 2:3, :] - m_t) for i in range(count)], jnp.add)
            target(b, m_s, l_s, m_t, l_t)

    def into(slots, me):
        def put(b, *values):
            for r, value in enumerate(values):
                slots[me, b, r : r + 1, :] = value

        return put

    s_x = [remote(sx.at[x], sx.at[x], sxs.at[o - 1], sxr.at[o - 1], at_x(o)) for o in range(1, NX)]
    s_y = [remote(sy.at[y], sy.at[y], sys_.at[o - 1], syr.at[o - 1], at_y(o)) for o in range(1, NY)]
    s_z = [remote(sz.at[z], sz.at[z], szs.at[o - 1], szr.at[o - 1], at_z(o)) for o in range(1, NZ)]
    for cp in s_y:
        cp.start()
    for cp in s_y:
        cp.wait_recv()
    reduce_stats(sy, NY, into(sz, z))
    for cp in s_z:
        cp.start()
    for cp in s_z:
        cp.wait_recv()
    reduce_stats(sz, NZ, into(sx, x))
    for cp in s_x:
        cp.start()
    for cp in s_x:
        cp.wait_recv()
    def columns(b, m_s, l_s, m_t, l_t):
        for r, value in enumerate((m_s, loss_scale / l_s, m_t, loss_scale / l_t)):
            col[r, b] = jnp.broadcast_to(value, (BLK, BLK)).T
        last[b, 0:1, :] = m_s + jnp.log(l_s) - m_t - jnp.log(l_t)
        last[b, 1:2, :] = l_t

    reduce_stats(sx, NX, columns)

    own_t.wait()
    for cp in t_x:
        cp.wait_recv()

    def rows_at(s, plane):
        turn = STEPS[s][0]
        k = lax.rem(y + turn, NY) if plane == 0 else lax.rem(y + NY - turn, NY)
        return pl.ds(pl.multiple_of(k * SUB + STEPS[s][1], 16), STEPS[s][2])

    def rows_mine(s):
        turn = STEPS[s][0]
        k = lax.rem(y + turn + c * (2 * NY - 2 * turn), NY)
        return pl.ds(pl.multiple_of(k * SUB + STEPS[s][1], 16), STEPS[s][2])

    def piece(s, owner, part, parts):
        size = NX * STEPS[s][2]
        first = FIRST[s] + c * size + part * (size // parts)
        return gbuf.at[pl.ds(pl.multiple_of(first, 32), size // parts), cols_of(owner)]

    left, right, far = lax.rem(x + 3, NX), lax.rem(x + 1, NX), lax.rem(x + 2, NX)
    owners = [x, left, far, right]
    g_a, g_f, g_c = [], [], []
    for s in range(len(STEPS)):
        own, low, high = piece(s, x, 0, 1), piece(s, left, 0, 2), piece(s, right, 1, 2)
        g_a.append([remote(own, own, gas.at[s, i], gar.at[s, i], at_x(o)) for i, o in enumerate((1, 3))])
        g_f.append(
            [
                remote(low, low, gfs.at[s, 0], gfr.at[s, 0], at_x(1)),
                remote(high, high, gfs.at[s, 1], gfr.at[s, 1], at_x(3)),
            ]
        )
        blocks = [piece(s, q, 0, 1) for q in owners]
        g_c.append([remote(q, q, gcs.at[s, o], gcr.at[s, o], other) for o, q in enumerate(blocks)])

    def make(s):
        rows, count = rows_mine(s), STEPS[s][2]

        def grad(b, carry):
            m_s, a_s, m_t, a_t = [col[r, b, rows, :] for r in range(4)]
            out = pl.ds(pl.multiple_of(FIRST[s] + c * (NX * count) + b * count, 16), count)
            total = jnp.zeros((count, 128), F32)
            tiles = []
            for g in range(PART // 128):
                st = student[b, rows, 128 * g : 128 * g + 128]
                te = tc[b, rows, 128 * g : 128 * g + 128]
                e_t = jnp.exp(te - m_t)
                total += e_t * (te - st)
                tiles.append((jnp.exp(st - m_s) * a_s - e_t * a_t).astype(BF16))
            gbuf[out, cols_of(x)] = jnp.concatenate(tiles, axis=1)
            cross[b, rows, :] = total
            return carry

        lax.fori_loop(0, NX, grad, 0)

    def offer(s):
        for cp in g_a[s]:
            cp.start()
        g_c[s][0].start()

    def pass_on(s):
        for i, o in enumerate((1, 3)):
            g_a[s][i].wait_recv()
            g_f[s][i].start()
            g_c[s][o].start()

    make(0)
    offer(0)
    make(1)
    offer(1)
    for s in range(2, len(STEPS)):
        make(s)

    keep.wait()
    h_c.wait_recv()
    for s in range(len(STEPS)):
        count = STEPS[s][2]
        block = jnp.concatenate([hx[j, b, rows_at(s, j), :] for j in range(2) for b in range(NX)], axis=0)
        block = pltpu.roll(block.astype(F32), lax.rem(c * WID, CHIP), 1)[:, :512]
        ht[:, FIRST[s] : FIRST[s] + 2 * NX * count] = block.T[:WID].astype(BF16)

    for b in range(NX):
        cx[x, b] = jnp.broadcast_to(row_sum(cross[b]), (8, BLK))
    c_x = [
        remote(
            cx.at[x, lax.rem(x + o, NX)], cx.at[x, lax.rem(x + o, NX)], cxs.at[o - 1], cxr.at[o - 1], at_x(o)
        )
        for o in range(1, NX)
    ]
    c_y = [remote(cy.at[y], cy.at[y], cys.at[o - 1], cyr.at[o - 1], at_y(o)) for o in range(1, NY)]
    c_z = [remote(cz.at[z], cz.at[z], czs.at[o - 1], czr.at[o - 1], at_z(o)) for o in range(1, NZ)]

    h_to_y = [
        [
            remote(
                hgp.at[s, pl.ds(j * BLK, BLK)], hgy.at[s, pl.ds(j * BLK, BLK)],
                hgys.at[s, j], hgyr.at[s, j], at_y(s + 1 if j == 0 else 3 - s),
            )
            for j in range(2)
        ]
        for s in range(NY - 1)
    ]

    def z_rows(i, o):
        zz = lax.rem(z + o, NZ)
        return pl.ds(pl.multiple_of(i * BLK + (zz % 2) * 64 + (zz // 2) * 16, 16), 16)

    h_to_z = [
        [
            remote(
                hgp.at[3, z_rows(i, o)], hgz.at[o - 1, pl.ds(16 * i, 16)], hgzs.at[i, o - 1], hgzr.at[i, o - 1], at_z(o)
            )
            for o in range(1, NZ)
        ]
        for i in range(2)
    ]

    def complete(s):
        for cp in g_f[s]:
            cp.wait_recv()
        g_c[s][2].start()
        for cp in g_c[s]:
            cp.wait_recv()
        size = 2 * NX * STEPS[s][2]
        product = jnp.dot(gbuf[FIRST[s] : FIRST[s] + size], wt[...], preferred_element_type=F32)
        if s < 3:
            hgp[s] = product
            for cp in h_to_y[s]:
                cp.start()
            return
        i = s - 3
        if i == 0:
            for cp in sum(h_to_y, []):
                cp.wait_recv()
        for j in range(2):
            for b in range(NX):
                rows = slice(j * BLK + b * SUB + 16 * i, j * BLK + b * SUB + 16 * i + 16)
                at = slice(j * 64 + b * 16, j * 64 + b * 16 + 16)
                out = slice(i * BLK + at.start, i * BLK + at.stop)
                hgp[3, out] = product[at] + hgy[0, rows] + hgy[1, rows] + hgy[2, rows]
        for cp in h_to_z[i]:
            cp.start()

    def head_product(s):
        depth = slice(BIG * s, BIG * s + BIG)

        def head(i, carry):
            cols = pl.ds(pl.multiple_of(i * 512, 512), 512)
            tile = jnp.dot(ht[:, depth], gbuf[depth, cols], preferred_element_type=F32)
            if s == 0:
                acc[:, cols] = tile
            elif s < 3:
                acc[:, cols] += tile
            else:
                dw_ref[:, cols] = (acc[:, cols] + tile).astype(BF16)
            return carry

        lax.fori_loop(0, COLS // 512, head, 0)

    pass_on(0)
    offer(2)
    pass_on(1)
    offer(3)
    for cp in c_x:
        cp.start()
    complete(0)
    head_product(0)
    pass_on(2)
    offer(4)
    for cp in c_x:
        cp.wait_recv()
    cy[y] = cx[0, x] + cx[1, x] + cx[2, x] + cx[3, x]
    for cp in c_y:
        cp.start()
    complete(1)
    head_product(1)
    pass_on(3)
    for cp in c_y:
        cp.wait_recv()
    cz[z] = cy[0] + cy[1] + cy[2] + cy[3]
    for cp in c_z:
        cp.start()
    complete(2)
    head_product(2)
    pass_on(4)
    complete(3)
    complete(4)
    head_product(3)

    for cp in c_z:
        cp.wait_recv()
    crossed = fold([cz[i, 0:1, :] for i in range(NZ)], jnp.add)
    div_ref[...] = crossed / last[x, 1:2, :] + last[x, 0:1, :]

    for i in range(2):
        for cp in h_to_z[i]:
            cp.wait_recv()
        total = hgp[3, z_rows(i, 0), :]
        for o in range(NZ - 1):
            total = total + hgz[o, 16 * i : 16 * i + 16]
        hg_ref[16 * i : 16 * i + 16, :] = total.astype(BF16)

    sent = h_x + [h_z, h_c] + w_c + t_x + s_x + s_y + s_z + c_x + c_y + c_z
    for cp in sent + sum(h_y + g_a + g_f + g_c + h_to_y + h_to_z, []):
        cp.wait_send()


def put(div_in, hg_in, dw_in, div_ref, hg_ref, dw_ref, sems):
    rows = WID // 7
    parts = [pl.ds(rows * i, rows) for i in range(7)]
    copies = [pltpu.make_async_copy(dw_in.at[p], dw_ref.at[p], sems.at[i]) for i, p in enumerate(parts)]
    for cp in copies:
        cp.start()
    div_ref[...] = div_in[0]
    hg_ref[...] = hg_in[...]
    for cp in copies:
        cp.wait()


def local(hidden, head_weight, teacher_logits):
    dma = pltpu.SemaphoreType.DMA
    vmem = pltpu.VMEM
    scratch = [
        vmem((NX, BLK, D), BF16),
        vmem((D, PART), BF16),
        vmem((NX, BLK, PART), F32),
        vmem((NX, BLK, PART), F32),
        vmem((BLK, COLS), F32),
        vmem((WID, COLS), BF16),
        vmem((COLS, WID), BF16),
        vmem((2, NX, BLK, CHIP), BF16),
        vmem((WID, ROWS), BF16),
        vmem((ROWS, COLS), BF16),
        vmem((WID, COLS), F32),
        vmem((NY, 2 * BLK, WID), F32),
        vmem((NY - 1, 2 * BLK, WID), F32),
        vmem((NZ - 1, SUB, WID), F32),
        vmem((NX, NX, 8, BLK), F32),
        vmem((NY, NX, 8, BLK), F32),
        vmem((NZ, NX, 8, BLK), F32),
        vmem((NX, 8, BLK), F32),
        vmem((4, NX, BLK, BLK), F32),
        vmem((NX, BLK, BLK), F32),
        vmem((NX, NX, 8, BLK), F32),
        vmem((NY, 8, BLK), F32),
        vmem((NZ, 8, BLK), F32),
    ]
    counts = [(3,), (1,), (2, 3), (3,), (4,), (3,), (1,), (3,), (3,), (7,)]
    counts += [(5, 2), (5, 2), (5, 4), (3, 2), (2, 7), (3,), (3,), (7,)]
    sems = [dma((6,))]
    for n in counts:
        sems += [dma(n), dma(n)]
    div, hg, dw = pl.pallas_call(
        kernel,
        name="distill",
        out_shape=(vmem((1, BLK), F32), vmem((SUB, WID), BF16), vmem((WID, COLS), BF16)),
        in_specs=[pl.BlockSpec(memory_space=pl.ANY)] * 3,
        out_specs=[pl.BlockSpec(memory_space=vmem)] * 3,
        scratch_shapes=scratch + sems,
        compiler_params=pltpu.CompilerParams(
            collective_id=0, has_side_effects=True, vmem_limit_bytes=54 * 1024 * 1024
        ),
    )(hidden, head_weight, teacher_logits)
    div, hg, dw = pl.pallas_call(
        put,
        name="put",
        out_shape=(
            jax.ShapeDtypeStruct((BLK,), F32),
            jax.ShapeDtypeStruct((SUB, WID), BF16),
            jax.ShapeDtypeStruct((WID, COLS), BF16),
        ),
        in_specs=[pl.BlockSpec(memory_space=vmem)] * 3,
        out_specs=[pl.BlockSpec(memory_space=vmem)] * 2 + [pl.BlockSpec(memory_space=pl.ANY)],
        scratch_shapes=[dma((7,))],
    )(div, hg, dw)
    return div, hg, dw


def solution(mesh):
    return jax.shard_map(
        local,
        mesh=mesh,
        in_specs=(P("dp", None), P("dp", "vocab"), P("dp", "vocab")),
        out_specs=(P("dp"), P("vocab", "dp"), P("dp", "vocab")),
        check_vma=False,
    )
```

```python
import jax
import jax.numpy as jnp
from jax import lax
from jax.experimental import pallas as pl
from jax.experimental.pallas import tpu as pltpu
from jax.sharding import PartitionSpec as P

MESH = pl.DeviceIdType.MESH
F32, BF16 = jnp.float32, jnp.bfloat16
loss_scale = 256.0
LOW = -3.0e38

D, ROWS = 3584, 1024
NX, NY, NZ = 4, 4, 8
BLK = 128
SUB = BLK // NY
WID = D // 8
CHIP = 2 * WID
COLS = 4096
PART = COLS // NX
HSH = D // NY
HALF = BLK // 2


STEPS = tuple((turn, first, 16) for first in (0, 16) for turn in (1, 2, 3, 0))
FIRST = tuple(128 * s for s in range(8))
EARLY = 112
WIDE = 512
AHEAD = 3


def groups(value):
    return [value[:, 128 * g : 128 * g + 128] for g in range(value.shape[1] // 128)]


def fold(parts, op):
    while len(parts) > 1:
        parts = [op(parts[i], parts[i + 1]) for i in range(0, len(parts), 2)]
    return parts[0]


def row_max(part):
    return jnp.max(part.T, axis=0, keepdims=True)


def row_sum(part):
    return jnp.sum(part.T, axis=0, keepdims=True)


def kernel(
    h_ref, w_ref, t_ref,
    div_ref, hg_ref, dw_ref,
    hc, wc, tc, student, town, wown, wt, hx, ht, gbuf, acc,
    hgp, hgy, hgz, sx, sy, sz, last, col, cross, cx, cy, cz,
    lsem, hxs, hxr, hzs, hzr, hys, hyr, wxs, wxr, wcs, wcr, ts, tr, hcs, hcr,
    sxs, sxr, sys_, syr, szs, szr, gas, gar, gfs, gfr, gcs, gcr,
    hgys, hgyr, hgzs, hgzr, cxs, cxr, cys, cyr, czs, czr,
):
    dp, v = lax.axis_index("dp"), lax.axis_index("vocab")
    x, c = dp // 2, dp % 2
    z, y = v // NY, v % NY

    def at_x(o):
        return (lax.rem(x + o, NX) * 2 + c, v)

    def at_y(o):
        return (dp, z * NY + lax.rem(y + o, NY))

    def at_z(o):
        return (dp, lax.rem(z + o, NZ) * NY + y)

    other = (x * 2 + 1 - c, v)
    beside = (dp, (z + 1 - 2 * (z % 2)) * NY + y)

    def remote(src, dst, ss, rs, device):
        return pltpu.make_async_remote_copy(
            src_ref=src, dst_ref=dst, send_sem=ss, recv_sem=rs, device_id=device, device_id_type=MESH
        )

    barrier = pltpu.get_barrier_semaphore()
    partners = [at_x(o) for o in range(1, NX)] + [other]
    partners += [at_y(o) for o in range(1, NY)] + [at_z(o) for o in range(1, NZ)]
    for p in partners:
        pl.semaphore_signal(barrier, inc=1, device_id=p, device_id_type=MESH)

    def cols_of(i):
        return pl.ds(pl.multiple_of(i * PART, PART), PART)

    def wrows(i, j):
        return pl.ds(pl.multiple_of(i * CHIP + j * WID, 64), WID)

    own_w = pltpu.make_async_copy(w_ref.at[:, cols_of(x)], wc.at[wrows(x, c)], lsem.at[0])
    share = pl.ds(pl.multiple_of(y * HSH, HSH), HSH)
    half_of = [pl.ds(pl.multiple_of((z % 2) * HALF, HALF), HALF), pl.ds(pl.multiple_of((1 - z % 2) * HALF, HALF), HALF)]
    own_h = pltpu.make_async_copy(h_ref.at[half_of[0], share], hc.at[x, half_of[0], share], lsem.at[1])
    own_t = pltpu.make_async_copy(t_ref.at[:, cols_of(x)], tc.at[x], lsem.at[2])
    all_t = pltpu.make_async_copy(t_ref, town, lsem.at[3])
    all_w = pltpu.make_async_copy(w_ref, wown.at[pl.ds(0, WID)], lsem.at[4])
    for cp in (own_h, all_t, all_w, own_w, own_t):
        cp.start()
    pl.semaphore_wait(barrier, len(partners))

    h_x = [
        remote(
            h_ref.at[half_of[0], share], hc.at[x, half_of[0], share], hxs.at[o - 1], hxr.at[o - 1], at_x(o)
        )
        for o in range(1, NX)
    ]
    w_x = [
        remote(
            w_ref.at[:, cols_of(lax.rem(x + o, NX))], wc.at[wrows(x, c)], wxs.at[o - 1], wxr.at[o - 1], at_x(o)
        )
        for o in range(1, NX)
    ]
    t_x = [
        [
            remote(
                t_ref.at[rows, cols_of(lax.rem(x + o, NX))], tc.at[x, rows], ts.at[i, o - 1], tr.at[i, o - 1], at_x(o)
            )
            for o in range(1, NX)
        ]
        for i, rows in enumerate((pl.ds(0, EARLY), pl.ds(EARLY, BLK - EARLY)))
    ]

    def w_core(o):
        rows = wrows(lax.rem(x + NX - o, NX), c)
        src = w_ref.at[:, cols_of(x)] if o == 0 else wc.at[rows]
        return remote(src, wc.at[rows], wcs.at[o], wcr.at[o], other)

    w_c = [w_core(o) for o in range(NX)]
    for cp in h_x + w_x:
        cp.start()
    w_c[0].start()

    own_h.wait()
    for cp in h_x:
        cp.wait_recv()
    shares = [hc.at[:, rows, share] for rows in half_of]
    h_z = remote(shares[0], shares[0], hzs.at[0], hzr.at[0], beside)
    h_y = [
        [remote(part, part, hys.at[i, o - 1], hyr.at[i, o - 1], at_y(o)) for o in range(1, NY)]
        for i, part in enumerate(shares)
    ]
    h_z.start()
    for cp in h_y[0]:
        cp.start()

    for b in range(NX):
        sy[y, b] = jnp.where(lax.broadcasted_iota(jnp.int32, (8, BLK), 0) % 2 == 0, LOW, 0.0)
    all_t.wait()
    part = fold([town[:, 128 * g : 128 * g + 128] for g in range(COLS // 128)], jnp.maximum)
    top = jnp.max(part, axis=1, keepdims=True)
    total = fold([jnp.exp(town[:, 128 * g : 128 * g + 128] - top) for g in range(COLS // 128)], jnp.add)
    sy[y, x, 2:3, :] = row_max(part)
    sy[y, x, 3:4, :] = row_sum(total)

    all_w.wait()
    wown[WID:] = jnp.zeros((WIDE - WID, COLS), BF16)

    def turn(i, carry):
        cols = pl.ds(pl.multiple_of(i * 512, 512), 512)
        wt[cols, :] = wown[:, cols].T
        return carry

    lax.fori_loop(0, COLS // 512, turn, 0)

    h_z.wait_recv()
    for cp in h_y[1]:
        cp.start()
    for o in (1, 3, 2):
        w_x[o - 1].wait_recv()
        w_c[o].start()
    for cp in w_x:
        cp.wait_send()
    for cp in t_x[0]:
        cp.start()
    for cp in h_y[0] + h_y[1]:
        cp.wait_recv()

    mine = pl.ds(pl.multiple_of(x * CHIP, CHIP), CHIP)
    h_c = remote(hc.at[:, :, mine], hx.at[c], hcs.at[0], hcr.at[0], other)
    h_c.start()
    keep = pltpu.make_async_copy(hc.at[:, :, mine], hx.at[c], lsem.at[5])
    keep.start()
    own_w.wait()
    for cp in w_c:
        cp.wait_recv()

    def score(i, carry):
        cols = pl.ds(pl.multiple_of(i * 256, 256), 256)
        tile = jnp.dot(hc[...].reshape(NX * BLK, D), wc[:, cols], preferred_element_type=F32)
        student[:, :, cols] = tile.reshape(NX, BLK, 256)
        return carry

    lax.fori_loop(0, PART // 256, score, 0)

    def local_stats(b, carry):
        parts = groups(student[b])
        part = fold(parts, jnp.maximum)
        top = jnp.max(part, axis=1, keepdims=True)
        total = fold([jnp.exp(p - top) for p in parts], jnp.add)
        sy[y, b, 0:1, :] = row_max(part)
        sy[y, b, 1:2, :] = row_sum(total)
        return carry

    lax.fori_loop(0, NX, local_stats, 0)

    def reduce_stats(slots, count, target):
        for b in range(NX):
            m_s = fold([slots[i, b, 0:1, :] for i in range(count)], jnp.maximum)
            m_t = fold([slots[i, b, 2:3, :] for i in range(count)], jnp.maximum)
            l_s = fold([slots[i, b, 1:2, :] * jnp.exp(slots[i, b, 0:1, :] - m_s) for i in range(count)], jnp.add)
            l_t = fold([slots[i, b, 3:4, :] * jnp.exp(slots[i, b, 2:3, :] - m_t) for i in range(count)], jnp.add)
            target(b, m_s, l_s, m_t, l_t)

    def into(slots, me):
        def put(b, *values):
            for r, value in enumerate(values):
                slots[me, b, r : r + 1, :] = value

        return put

    s_x = [remote(sx.at[x], sx.at[x], sxs.at[o - 1], sxr.at[o - 1], at_x(o)) for o in range(1, NX)]
    s_y = [remote(sy.at[y], sy.at[y], sys_.at[o - 1], syr.at[o - 1], at_y(o)) for o in range(1, NY)]
    s_z = [remote(sz.at[z], sz.at[z], szs.at[o - 1], szr.at[o - 1], at_z(o)) for o in range(1, NZ)]
    for cp in s_y:
        cp.start()
    for cp in s_y:
        cp.wait_recv()
    reduce_stats(sy, NY, into(sz, z))
    for cp in s_z:
        cp.start()
    for cp in s_z:
        cp.wait_recv()
    reduce_stats(sz, NZ, into(sx, x))
    for cp in s_x + t_x[1]:
        cp.start()
    for cp in s_x:
        cp.wait_recv()
    def columns(b, m_s, l_s, m_t, l_t):
        for r, value in enumerate((m_s, loss_scale / l_s, m_t, loss_scale / l_t)):
            col[r, b] = jnp.broadcast_to(value, (BLK, BLK)).T
        last[b, 0:1, :] = m_s + jnp.log(l_s) - m_t - jnp.log(l_t)
        last[b, 1:2, :] = l_t

    reduce_stats(sx, NX, columns)

    own_t.wait()
    for cp in t_x[0] + t_x[1]:
        cp.wait_recv()

    def rows_at(s, plane):
        turn = STEPS[s][0]
        k = lax.rem(y + turn, NY) if plane == 0 else lax.rem(y + NY - turn, NY)
        return pl.ds(pl.multiple_of(k * SUB + STEPS[s][1], 16), STEPS[s][2])

    def rows_mine(s):
        turn = STEPS[s][0]
        k = lax.rem(y + turn + c * (2 * NY - 2 * turn), NY)
        return pl.ds(pl.multiple_of(k * SUB + STEPS[s][1], 16), STEPS[s][2])

    def piece(s, owner, part, parts):
        size = NX * STEPS[s][2]
        first = FIRST[s] + c * size + part * (size // parts)
        return gbuf.at[pl.ds(pl.multiple_of(first, 32), size // parts), cols_of(owner)]

    left, right, far = lax.rem(x + 3, NX), lax.rem(x + 1, NX), lax.rem(x + 2, NX)
    owners = [x, left, far, right]
    g_a, g_f, g_c = [], [], []
    for s in range(len(STEPS)):
        own, low, high = piece(s, x, 0, 1), piece(s, left, 0, 2), piece(s, right, 1, 2)
        g_a.append([remote(own, own, gas.at[s, i], gar.at[s, i], at_x(o)) for i, o in enumerate((1, 3))])
        g_f.append(
            [
                remote(low, low, gfs.at[s, 0], gfr.at[s, 0], at_x(1)),
                remote(high, high, gfs.at[s, 1], gfr.at[s, 1], at_x(3)),
            ]
        )
        blocks = [piece(s, q, 0, 1) for q in owners]
        g_c.append([remote(q, q, gcs.at[s, o], gcr.at[s, o], other) for o, q in enumerate(blocks)])

    def make(s):
        rows, count = rows_mine(s), STEPS[s][2]

        def grad(b, carry):
            m_s, a_s, m_t, a_t = [col[r, b, rows, :] for r in range(4)]
            out = pl.ds(pl.multiple_of(FIRST[s] + c * (NX * count) + b * count, 16), count)
            total = jnp.zeros((count, 128), F32)
            tiles = []
            for g in range(PART // 128):
                st = student[b, rows, 128 * g : 128 * g + 128]
                te = tc[b, rows, 128 * g : 128 * g + 128]
                e_t = jnp.exp(te - m_t)
                total += e_t * (te - st)
                tiles.append((jnp.exp(st - m_s) * a_s - e_t * a_t).astype(BF16))
            gbuf[out, cols_of(x)] = jnp.concatenate(tiles, axis=1)
            cross[b, rows, :] = total
            return carry

        lax.fori_loop(0, NX, grad, 0)

    def offer(s):
        for cp in g_a[s]:
            cp.start()
        g_c[s][0].start()

    def pass_on(s):
        for i, o in enumerate((1, 3)):
            g_a[s][i].wait_recv()
            g_f[s][i].start()
            g_c[s][o].start()

    for s in range(len(STEPS)):
        make(s)
        if s < AHEAD:
            offer(s)

    keep.wait()
    h_c.wait_recv()
    for s in range(len(STEPS)):
        count = STEPS[s][2]
        block = jnp.concatenate([hx[j, b, rows_at(s, j), :] for j in range(2) for b in range(NX)], axis=0)
        block = pltpu.roll(block.astype(F32), lax.rem(c * WID, CHIP), 1)[:, :512]
        ht[:, FIRST[s] : FIRST[s] + 2 * NX * count] = block.T[:WID].astype(BF16)

    for b in range(NX):
        cx[x, b] = jnp.broadcast_to(row_sum(cross[b]), (8, BLK))
    c_x = [
        remote(
            cx.at[x, lax.rem(x + o, NX)], cx.at[x, lax.rem(x + o, NX)], cxs.at[o - 1], cxr.at[o - 1], at_x(o)
        )
        for o in range(1, NX)
    ]
    c_y = [remote(cy.at[y], cy.at[y], cys.at[o - 1], cyr.at[o - 1], at_y(o)) for o in range(1, NY)]
    c_z = [remote(cz.at[z], cz.at[z], czs.at[o - 1], czr.at[o - 1], at_z(o)) for o in range(1, NZ)]

    def to_y(s, j):
        rows = pl.ds(s * BLK + j * 64, 64)
        up = STEPS[s][0] if j == 0 else NY - STEPS[s][0]
        return remote(hgp.at[rows], hgy.at[rows], hgys.at[s, j], hgyr.at[s, j], at_y(up))

    def to_z(i, o):
        zz = lax.rem(z + o, NZ)
        rows = pl.ds(pl.multiple_of((4 * i + 3) * BLK + (zz % 2) * 64 + (zz // 2) * 16, 16), 16)
        return remote(hgp.at[rows], hgz.at[o - 1, pl.ds(16 * i, 16)], hgzs.at[i, o - 1], hgzr.at[i, o - 1], at_z(o))

    h_to_y = [[to_y(s, j) for j in range(2)] if STEPS[s][0] else [] for s in range(len(STEPS))]
    h_to_z = [[to_z(i, o) for o in range(1, NZ)] for i in range(2)]

    def far_in(s):
        for cp in g_f[s]:
            cp.wait_recv()
        g_c[s][2].start()

    def product(s):
        for cp in g_c[s]:
            cp.wait_recv()
        rows = slice(FIRST[s], FIRST[s] + BLK)
        hgp[rows] = jnp.dot(gbuf[rows], wt[...], preferred_element_type=F32)
        for cp in h_to_y[s]:
            cp.start()

    def gather_z(i):
        for cp in sum(h_to_y[4 * i : 4 * i + 3], []):
            cp.wait_recv()
        at = [slice((4 * i + t) * BLK, (4 * i + t + 1) * BLK) for t in range(4)]
        hgp[at[3]] += hgy[at[0]] + hgy[at[1]] + hgy[at[2]]
        for cp in h_to_z[i]:
            cp.start()

    def head_product(i, first, last):
        depth = slice(512 * i, 512 * i + 512)

        def head(n, carry):
            cols = pl.ds(pl.multiple_of(n * 512, 512), 512)
            tile = jnp.dot(ht[:, depth], gbuf[depth, cols], preferred_element_type=F32)
            if i == 0:
                acc[:, cols] = tile
            else:
                dw_ref[:, cols] = (acc[:, cols] + tile).astype(BF16)
            return carry

        lax.fori_loop(first, last, head, 0)

    for s in range(len(STEPS)):
        pass_on(s)
        if s + AHEAD < len(STEPS):
            offer(s + AHEAD)
        if s == 1:
            for cp in c_x:
                cp.start()
        if s == 3:
            for cp in c_x:
                cp.wait_recv()
            cy[y] = cx[0, x] + cx[1, x] + cx[2, x] + cx[3, x]
            for cp in c_y:
                cp.start()
        if s == 5:
            for cp in c_y:
                cp.wait_recv()
            cz[z] = cy[0] + cy[1] + cy[2] + cy[3]
            for cp in c_z:
                cp.start()
        if s >= 3:
            product(s - 3)
        if s >= 2:
            far_in(s - 2)
    product(5)
    far_in(6)
    product(6)
    gather_z(0)
    far_in(7)
    product(7)
    gather_z(1)
    head_product(0, 0, 8)
    head_product(1, 0, 8)

    for cp in c_z:
        cp.wait_recv()
    crossed = fold([cz[i, 0:1, :] for i in range(NZ)], jnp.add)
    div_ref[...] = crossed / last[x, 1:2, :] + last[x, 0:1, :]

    for i in range(2):
        for cp in h_to_z[i]:
            cp.wait_recv()
        mine = pl.ds(pl.multiple_of((4 * i + 3) * BLK + (z % 2) * 64 + (z // 2) * 16, 16), 16)
        total = hgp[mine, :]
        for o in range(NZ - 1):
            total = total + hgz[o, 16 * i : 16 * i + 16]
        hg_ref[16 * i : 16 * i + 16, :] = total[:, :WID].astype(BF16)

    sent = h_x + [h_z, h_c] + w_c + s_x + s_y + s_z + c_x + c_y + c_z
    for cp in sent + sum(h_y + t_x + g_a + g_f + g_c + h_to_y + h_to_z, []):
        cp.wait_send()


def put(div_in, hg_in, dw_in, div_ref, hg_ref, dw_ref, sems):
    rows = WID // 7
    parts = [pl.ds(rows * i, rows) for i in range(7)]
    copies = [pltpu.make_async_copy(dw_in.at[p], dw_ref.at[p], sems.at[i]) for i, p in enumerate(parts)]
    for cp in copies:
        cp.start()
    div_ref[...] = div_in[0]
    hg_ref[...] = hg_in[...]
    for cp in copies:
        cp.wait()


def local(hidden, head_weight, teacher_logits):
    dma = pltpu.SemaphoreType.DMA
    vmem = pltpu.VMEM
    scratch = [
        vmem((NX, BLK, D), BF16),
        vmem((D, PART), BF16),
        vmem((NX, BLK, PART), F32),
        vmem((NX, BLK, PART), F32),
        vmem((BLK, COLS), F32),
        vmem((WIDE, COLS), BF16),
        vmem((COLS, WIDE), BF16),
        vmem((2, NX, BLK, CHIP), BF16),
        vmem((WID, ROWS), BF16),
        vmem((ROWS, COLS), BF16),
        vmem((WID, COLS), F32),
        vmem((ROWS, WIDE), F32),
        vmem((ROWS, WIDE), F32),
        vmem((NZ - 1, SUB, WIDE), F32),
        vmem((NX, NX, 8, BLK), F32),
        vmem((NY, NX, 8, BLK), F32),
        vmem((NZ, NX, 8, BLK), F32),
        vmem((NX, 8, BLK), F32),
        vmem((4, NX, BLK, BLK), F32),
        vmem((NX, BLK, BLK), F32),
        vmem((NX, NX, 8, BLK), F32),
        vmem((NY, 8, BLK), F32),
        vmem((NZ, 8, BLK), F32),
    ]
    counts = [(3,), (1,), (2, 3), (3,), (4,), (2, 3), (1,), (3,), (3,), (7,)]
    counts += [(8, 2), (8, 2), (8, 4), (8, 2), (2, 7), (3,), (3,), (7,)]
    sems = [dma((6,))]
    for n in counts:
        sems += [dma(n), dma(n)]
    div, hg, dw = pl.pallas_call(
        kernel,
        name="distill",
        out_shape=(vmem((1, BLK), F32), vmem((SUB, WID), BF16), vmem((WID, COLS), BF16)),
        in_specs=[pl.BlockSpec(memory_space=pl.ANY)] * 3,
        out_specs=[pl.BlockSpec(memory_space=vmem)] * 3,
        scratch_shapes=scratch + sems,
        compiler_params=pltpu.CompilerParams(
            collective_id=0, has_side_effects=True, vmem_limit_bytes=54 * 1024 * 1024
        ),
    )(hidden, head_weight, teacher_logits)
    div, hg, dw = pl.pallas_call(
        put,
        name="put",
        out_shape=(
            jax.ShapeDtypeStruct((BLK,), F32),
            jax.ShapeDtypeStruct((SUB, WID), BF16),
            jax.ShapeDtypeStruct((WID, COLS), BF16),
        ),
        in_specs=[pl.BlockSpec(memory_space=vmem)] * 3,
        out_specs=[pl.BlockSpec(memory_space=vmem)] * 2 + [pl.BlockSpec(memory_space=pl.ANY)],
        scratch_shapes=[dma((7,))],
        compiler_params=pltpu.CompilerParams(vmem_limit_bytes=2 * 1024 * 1024),
    )(div, hg, dw)
    return div, hg, dw


def solution(mesh):
    return jax.shard_map(
        local,
        mesh=mesh,
        in_specs=(P("dp", None), P("dp", "vocab"), P("dp", "vocab")),
        out_specs=(P("dp"), P("vocab", "dp"), P("dp", "vocab")),
        check_vma=False,
    )
```

```python
import jax
import jax.numpy as jnp
from jax import lax
from jax.experimental import pallas as pl
from jax.experimental.pallas import tpu as pltpu
from jax.sharding import PartitionSpec as P

MESH = pl.DeviceIdType.MESH
F32, BF16 = jnp.float32, jnp.bfloat16
loss_scale = 256.0
LOW = -3.0e38

D, ROWS = 3584, 1024
NX, NY, NZ = 4, 4, 8
BLK = 128
SUB = BLK // NY
WID = D // 8
CHIP = 2 * WID
COLS = 4096
PART = COLS // NX
HSH = D // NY
HALF = BLK // 2


STEPS = tuple((turn, first, 16) for turn, first in zip((3, 2, 3, 1, 2, 0, 1, 0), (0, 0, 16, 0, 16, 0, 16, 16)))
BEFORE = (None, 0, None, 1, 2, 3, 4, 6)
LAST = (5, 7)
FIRST = tuple(128 * s for s in range(8))
EARLY = 112
WIDE = 512
OFFERS = {0: 3, 2: 4, 3: 5, 4: 6, 6: 7}


def groups(value):
    return [value[:, 128 * g : 128 * g + 128] for g in range(value.shape[1] // 128)]


def fold(parts, op):
    while len(parts) > 1:
        parts = [op(parts[i], parts[i + 1]) for i in range(0, len(parts), 2)]
    return parts[0]


def row_max(part):
    return jnp.max(part.T, axis=0, keepdims=True)


def row_sum(part):
    return jnp.sum(part.T, axis=0, keepdims=True)


def kernel(
    h_ref, w_ref, t_ref,
    div_ref, hg_ref, dw_ref,
    hc, wc, tc, student, town, wown, wt, hx, ht, gbuf, acc,
    hgp, hgy, hgz, sx, sy, sz, last, col, cross, cx, cy, cz,
    lsem, hxs, hxr, hzs, hzr, hys, hyr, wxs, wxr, wcs, wcr, ts, tr, hcs, hcr,
    sxs, sxr, sys_, syr, szs, szr, gas, gar, gfs, gfr, gcs, gcr,
    hgys, hgyr, hgzs, hgzr, cxs, cxr, cys, cyr, czs, czr,
):
    dp, v = lax.axis_index("dp"), lax.axis_index("vocab")
    x, c = dp // 2, dp % 2
    z, y = v // NY, v % NY

    def at_x(o):
        return (lax.rem(x + o, NX) * 2 + c, v)

    def at_y(o):
        return (dp, z * NY + lax.rem(y + o, NY))

    def at_z(o):
        return (dp, lax.rem(z + o, NZ) * NY + y)

    other = (x * 2 + 1 - c, v)
    beside = (dp, (z + 1 - 2 * (z % 2)) * NY + y)

    def remote(src, dst, ss, rs, device):
        return pltpu.make_async_remote_copy(
            src_ref=src, dst_ref=dst, send_sem=ss, recv_sem=rs, device_id=device, device_id_type=MESH
        )

    barrier = pltpu.get_barrier_semaphore()
    partners = [at_x(o) for o in range(1, NX)] + [other]
    partners += [at_y(o) for o in range(1, NY)] + [at_z(o) for o in range(1, NZ)]
    for p in partners:
        pl.semaphore_signal(barrier, inc=1, device_id=p, device_id_type=MESH)

    def cols_of(i):
        return pl.ds(pl.multiple_of(i * PART, PART), PART)

    def wrows(i, j):
        return pl.ds(pl.multiple_of(i * CHIP + j * WID, 64), WID)

    own_w = pltpu.make_async_copy(w_ref.at[:, cols_of(x)], wc.at[wrows(x, c)], lsem.at[0])
    share = pl.ds(pl.multiple_of(y * HSH, HSH), HSH)
    half_of = [pl.ds(pl.multiple_of((z % 2) * HALF, HALF), HALF), pl.ds(pl.multiple_of((1 - z % 2) * HALF, HALF), HALF)]
    own_h = pltpu.make_async_copy(h_ref.at[half_of[0], share], hc.at[x, half_of[0], share], lsem.at[1])
    own_t = pltpu.make_async_copy(t_ref.at[:, cols_of(x)], tc.at[x], lsem.at[2])
    all_t = pltpu.make_async_copy(t_ref, town, lsem.at[3])
    all_w = pltpu.make_async_copy(w_ref, wown.at[pl.ds(0, WID)], lsem.at[4])
    for cp in (own_h, all_t, all_w, own_w, own_t):
        cp.start()
    pl.semaphore_wait(barrier, len(partners))

    h_x = [
        remote(
            h_ref.at[half_of[0], share], hc.at[x, half_of[0], share], hxs.at[o - 1], hxr.at[o - 1], at_x(o)
        )
        for o in range(1, NX)
    ]
    w_x = [
        remote(
            w_ref.at[:, cols_of(lax.rem(x + o, NX))], wc.at[wrows(x, c)], wxs.at[o - 1], wxr.at[o - 1], at_x(o)
        )
        for o in range(1, NX)
    ]
    t_x = [
        [
            remote(
                t_ref.at[rows, cols_of(lax.rem(x + o, NX))], tc.at[x, rows], ts.at[i, o - 1], tr.at[i, o - 1], at_x(o)
            )
            for o in range(1, NX)
        ]
        for i, rows in enumerate((pl.ds(0, EARLY), pl.ds(EARLY, BLK - EARLY)))
    ]

    def w_core(o):
        rows = wrows(lax.rem(x + NX - o, NX), c)
        src = w_ref.at[:, cols_of(x)] if o == 0 else wc.at[rows]
        return remote(src, wc.at[rows], wcs.at[o], wcr.at[o], other)

    w_c = [w_core(o) for o in range(NX)]
    for cp in h_x + w_x:
        cp.start()
    w_c[0].start()

    own_h.wait()
    for cp in h_x:
        cp.wait_recv()
    shares = [hc.at[:, rows, share] for rows in half_of]
    h_z = remote(shares[0], shares[0], hzs.at[0], hzr.at[0], beside)
    h_y = [
        [remote(part, part, hys.at[i, o - 1], hyr.at[i, o - 1], at_y(o)) for o in range(1, NY)]
        for i, part in enumerate(shares)
    ]
    h_z.start()
    for cp in h_y[0]:
        cp.start()

    for b in range(NX):
        sy[y, b] = jnp.where(lax.broadcasted_iota(jnp.int32, (8, BLK), 0) % 2 == 0, LOW, 0.0)
    all_t.wait()
    part = fold([town[:, 128 * g : 128 * g + 128] for g in range(COLS // 128)], jnp.maximum)
    top = jnp.max(part, axis=1, keepdims=True)
    total = fold([jnp.exp(town[:, 128 * g : 128 * g + 128] - top) for g in range(COLS // 128)], jnp.add)
    sy[y, x, 2:3, :] = row_max(part)
    sy[y, x, 3:4, :] = row_sum(total)

    all_w.wait()
    wown[WID:] = jnp.zeros((WIDE - WID, COLS), BF16)

    def turn(i, carry):
        cols = pl.ds(pl.multiple_of(i * 512, 512), 512)
        wt[cols, :] = wown[:, cols].T
        return carry

    lax.fori_loop(0, COLS // 512, turn, 0)

    h_z.wait_recv()
    for cp in h_y[1]:
        cp.start()
    for o in (1, 3, 2):
        w_x[o - 1].wait_recv()
        w_c[o].start()
    for cp in w_x:
        cp.wait_send()
    for cp in t_x[0]:
        cp.start()
    for cp in h_y[0] + h_y[1]:
        cp.wait_recv()

    mine = pl.ds(pl.multiple_of(x * CHIP, CHIP), CHIP)
    h_c = remote(hc.at[:, :, mine], hx.at[c], hcs.at[0], hcr.at[0], other)
    h_c.start()
    keep = pltpu.make_async_copy(hc.at[:, :, mine], hx.at[c], lsem.at[5])
    keep.start()
    own_w.wait()
    for cp in w_c:
        cp.wait_recv()

    def score(i, carry):
        cols = pl.ds(pl.multiple_of(i * 256, 256), 256)
        tile = jnp.dot(hc[...].reshape(NX * BLK, D), wc[:, cols], preferred_element_type=F32)
        student[:, :, cols] = tile.reshape(NX, BLK, 256)
        return carry

    lax.fori_loop(0, PART // 256, score, 0)

    def local_stats(b, carry):
        parts = groups(student[b])
        part = fold(parts, jnp.maximum)
        top = jnp.max(part, axis=1, keepdims=True)
        total = fold([jnp.exp(p - top) for p in parts], jnp.add)
        sy[y, b, 0:1, :] = row_max(part)
        sy[y, b, 1:2, :] = row_sum(total)
        return carry

    lax.fori_loop(0, NX, local_stats, 0)

    def reduce_stats(slots, count, target):
        for b in range(NX):
            m_s = fold([slots[i, b, 0:1, :] for i in range(count)], jnp.maximum)
            m_t = fold([slots[i, b, 2:3, :] for i in range(count)], jnp.maximum)
            l_s = fold([slots[i, b, 1:2, :] * jnp.exp(slots[i, b, 0:1, :] - m_s) for i in range(count)], jnp.add)
            l_t = fold([slots[i, b, 3:4, :] * jnp.exp(slots[i, b, 2:3, :] - m_t) for i in range(count)], jnp.add)
            target(b, m_s, l_s, m_t, l_t)

    def into(slots, me):
        def put(b, *values):
            for r, value in enumerate(values):
                slots[me, b, r : r + 1, :] = value

        return put

    s_x = [remote(sx.at[x], sx.at[x], sxs.at[o - 1], sxr.at[o - 1], at_x(o)) for o in range(1, NX)]
    s_y = [remote(sy.at[y], sy.at[y], sys_.at[o - 1], syr.at[o - 1], at_y(o)) for o in range(1, NY)]
    s_z = [remote(sz.at[z], sz.at[z], szs.at[o - 1], szr.at[o - 1], at_z(o)) for o in range(1, NZ)]
    for cp in s_y:
        cp.start()
    for cp in s_y:
        cp.wait_recv()
    reduce_stats(sy, NY, into(sz, z))
    for cp in s_z:
        cp.start()
    for cp in s_z:
        cp.wait_recv()
    reduce_stats(sz, NZ, into(sx, x))
    for cp in s_x + t_x[1]:
        cp.start()
    for cp in s_x:
        cp.wait_recv()
    def columns(b, m_s, l_s, m_t, l_t):
        for r, value in enumerate((m_s, loss_scale / l_s, m_t, loss_scale / l_t)):
            col[r, b] = jnp.broadcast_to(value, (BLK, BLK)).T
        last[b, 0:1, :] = m_s + jnp.log(l_s) - m_t - jnp.log(l_t)
        last[b, 1:2, :] = l_t

    reduce_stats(sx, NX, columns)

    own_t.wait()
    for cp in t_x[0] + t_x[1]:
        cp.wait_recv()

    def rows_at(s, plane):
        turn = STEPS[s][0]
        k = lax.rem(y + turn, NY) if plane == 0 else lax.rem(y + NY - turn, NY)
        return pl.ds(pl.multiple_of(k * SUB + STEPS[s][1], 16), STEPS[s][2])

    def rows_mine(s):
        turn = STEPS[s][0]
        k = lax.rem(y + turn + c * (2 * NY - 2 * turn), NY)
        return pl.ds(pl.multiple_of(k * SUB + STEPS[s][1], 16), STEPS[s][2])

    def piece(s, owner, part, parts):
        size = NX * STEPS[s][2]
        first = FIRST[s] + c * size + part * (size // parts)
        return gbuf.at[pl.ds(pl.multiple_of(first, 32), size // parts), cols_of(owner)]

    left, right, far = lax.rem(x + 3, NX), lax.rem(x + 1, NX), lax.rem(x + 2, NX)
    owners = [x, left, far, right]
    g_a, g_f, g_c = [], [], []
    for s in range(len(STEPS)):
        own, low, high = piece(s, x, 0, 1), piece(s, left, 0, 2), piece(s, right, 1, 2)
        g_a.append([remote(own, own, gas.at[s, i], gar.at[s, i], at_x(o)) for i, o in enumerate((1, 3))])
        g_f.append(
            [
                remote(low, low, gfs.at[s, 0], gfr.at[s, 0], at_x(1)),
                remote(high, high, gfs.at[s, 1], gfr.at[s, 1], at_x(3)),
            ]
        )
        blocks = [piece(s, q, 0, 1) for q in owners]
        g_c.append([remote(q, q, gcs.at[s, o], gcr.at[s, o], other) for o, q in enumerate(blocks)])

    def make(s):
        rows, count = rows_mine(s), STEPS[s][2]

        def grad(b, carry):
            m_s, a_s, m_t, a_t = [col[r, b, rows, :] for r in range(4)]
            out = pl.ds(pl.multiple_of(FIRST[s] + c * (NX * count) + b * count, 16), count)
            total = jnp.zeros((count, 128), F32)
            tiles = []
            for g in range(PART // 128):
                st = student[b, rows, 128 * g : 128 * g + 128]
                te = tc[b, rows, 128 * g : 128 * g + 128]
                e_t = jnp.exp(te - m_t)
                total += e_t * (te - st)
                tiles.append((jnp.exp(st - m_s) * a_s - e_t * a_t).astype(BF16))
            gbuf[out, cols_of(x)] = jnp.concatenate(tiles, axis=1)
            cross[b, rows, :] = total
            return carry

        lax.fori_loop(0, NX, grad, 0)

    def offer(s):
        for cp in g_a[s]:
            cp.start()
        g_c[s][0].start()

    def pass_on(s):
        for i, o in enumerate((1, 3)):
            g_a[s][i].wait_recv()
            g_f[s][i].start()
            g_c[s][o].start()

    make(0)
    offer(0)
    for s in range(1, len(STEPS)):
        make(s)
    for b in range(NX):
        cx[x, b] = jnp.broadcast_to(row_sum(cross[b]), (8, BLK))
    offer(1)

    keep.wait()
    h_c.wait_recv()
    for s in range(len(STEPS)):
        if s == 4:
            offer(2)
        count = STEPS[s][2]
        block = jnp.concatenate([hx[j, b, rows_at(s, j), :] for j in range(2) for b in range(NX)], axis=0)
        block = pltpu.roll(block.astype(F32), lax.rem(c * WID, CHIP), 1)[:, :512]
        ht[:, FIRST[s] : FIRST[s] + 2 * NX * count] = block.T[:WID].astype(BF16)

    c_x = [
        remote(
            cx.at[x, lax.rem(x + o, NX)], cx.at[x, lax.rem(x + o, NX)], cxs.at[o - 1], cxr.at[o - 1], at_x(o)
        )
        for o in range(1, NX)
    ]
    c_y = [remote(cy.at[y], cy.at[y], cys.at[o - 1], cyr.at[o - 1], at_y(o)) for o in range(1, NY)]
    c_z = [remote(cz.at[z], cz.at[z], czs.at[o - 1], czr.at[o - 1], at_z(o)) for o in range(1, NZ)]

    def to_y(s, j):
        rows = pl.ds(s * BLK + j * 64, 64)
        return remote(hgp.at[rows], hgy.at[rows], hgys.at[s, j], hgyr.at[s, j], at_y(NY - 1 if j else 1))

    def to_z(i, o):
        zz = lax.rem(z + o, NZ)
        rows = pl.ds(pl.multiple_of(LAST[i] * BLK + (zz % 2) * 64 + (zz // 2) * 16, 16), 16)
        return remote(hgp.at[rows], hgz.at[o - 1, pl.ds(16 * i, 16)], hgzs.at[i, o - 1], hgzr.at[i, o - 1], at_z(o))

    h_to_y = [[to_y(s, j) for j in range(2)] if STEPS[s][0] else [] for s in range(len(STEPS))]
    h_to_z = [[to_z(i, o) for o in range(1, NZ)] for i in range(2)]

    def far_in(s):
        for cp in g_f[s]:
            cp.wait_recv()
        g_c[s][2].start()

    def product(s):
        for cp in g_c[s]:
            cp.wait_recv()
        rows = slice(FIRST[s], FIRST[s] + BLK)
        hgp[rows] = jnp.dot(gbuf[rows], wt[...], preferred_element_type=F32)
        if BEFORE[s] is not None:
            for cp in h_to_y[BEFORE[s]]:
                cp.wait_recv()
            hgp[rows] += hgy[FIRST[BEFORE[s]] : FIRST[BEFORE[s]] + BLK]
        for cp in h_to_y[s] or h_to_z[LAST.index(s)]:
            cp.start()

    def head_product(i, first, last):
        depth = slice(512 * i, 512 * i + 512)

        def head(n, carry):
            cols = pl.ds(pl.multiple_of(n * 512, 512), 512)
            tile = jnp.dot(ht[:, depth], gbuf[depth, cols], preferred_element_type=F32)
            if i == 0:
                acc[:, cols] = tile
            else:
                dw_ref[:, cols] = (acc[:, cols] + tile).astype(BF16)
            return carry

        lax.fori_loop(first, last, head, 0)

    def near(s):
        pass_on(s)
        if s in OFFERS:
            offer(OFFERS[s])

    near(0)
    near(1)
    for cp in c_x:
        cp.start()
    near(2)
    far_in(0)
    product(0)
    far_in(1)
    near(3)
    far_in(2)
    product(1)
    for cp in c_x:
        cp.wait_recv()
    cy[y] = cx[0, x] + cx[1, x] + cx[2, x] + cx[3, x]
    for cp in c_y:
        cp.start()
    near(4)
    product(2)
    far_in(3)
    product(3)
    head_product(0, 0, 2)
    far_in(4)
    near(5)
    near(6)
    for cp in c_y:
        cp.wait_recv()
    cz[z] = cy[0] + cy[1] + cy[2] + cy[3]
    for cp in c_z:
        cp.start()
    product(4)
    far_in(5)
    head_product(0, 2, 4)
    product(5)
    far_in(6)
    near(7)
    product(6)
    head_product(0, 4, 6)
    far_in(7)
    product(7)
    head_product(0, 6, 8)
    head_product(1, 0, 8)

    for cp in c_z:
        cp.wait_recv()
    crossed = fold([cz[i, 0:1, :] for i in range(NZ)], jnp.add)
    div_ref[...] = crossed / last[x, 1:2, :] + last[x, 0:1, :]

    for i in range(2):
        for cp in h_to_z[i]:
            cp.wait_recv()
        mine = pl.ds(pl.multiple_of(LAST[i] * BLK + (z % 2) * 64 + (z // 2) * 16, 16), 16)
        total = hgp[mine, :]
        for o in range(NZ - 1):
            total = total + hgz[o, 16 * i : 16 * i + 16]
        hg_ref[16 * i : 16 * i + 16, :] = total[:, :WID].astype(BF16)

    sent = h_x + [h_z, h_c] + w_c + s_x + s_y + s_z + c_x + c_y + c_z
    for cp in sent + sum(h_y + t_x + g_a + g_f + g_c + h_to_y + h_to_z, []):
        cp.wait_send()


def put(div_in, hg_in, dw_in, div_ref, hg_ref, dw_ref, sems):
    rows = WID // 7
    parts = [pl.ds(rows * i, rows) for i in range(7)]
    copies = [pltpu.make_async_copy(dw_in.at[p], dw_ref.at[p], sems.at[i]) for i, p in enumerate(parts)]
    for cp in copies:
        cp.start()
    div_ref[...] = div_in[0]
    hg_ref[...] = hg_in[...]
    for cp in copies:
        cp.wait()


def local(hidden, head_weight, teacher_logits):
    dma = pltpu.SemaphoreType.DMA
    vmem = pltpu.VMEM
    scratch = [
        vmem((NX, BLK, D), BF16),
        vmem((D, PART), BF16),
        vmem((NX, BLK, PART), F32),
        vmem((NX, BLK, PART), F32),
        vmem((BLK, COLS), F32),
        vmem((WIDE, COLS), BF16),
        vmem((COLS, WIDE), BF16),
        vmem((2, NX, BLK, CHIP), BF16),
        vmem((WID, ROWS), BF16),
        vmem((ROWS, COLS), BF16),
        vmem((WID, COLS), F32),
        vmem((ROWS, WIDE), F32),
        vmem((ROWS, WIDE), F32),
        vmem((NZ - 1, SUB, WIDE), F32),
        vmem((NX, NX, 8, BLK), F32),
        vmem((NY, NX, 8, BLK), F32),
        vmem((NZ, NX, 8, BLK), F32),
        vmem((NX, 8, BLK), F32),
        vmem((4, NX, BLK, BLK), F32),
        vmem((NX, BLK, BLK), F32),
        vmem((NX, NX, 8, BLK), F32),
        vmem((NY, 8, BLK), F32),
        vmem((NZ, 8, BLK), F32),
    ]
    counts = [(3,), (1,), (2, 3), (3,), (4,), (2, 3), (1,), (3,), (3,), (7,)]
    counts += [(8, 2), (8, 2), (8, 4), (8, 2), (2, 7), (3,), (3,), (7,)]
    sems = [dma((6,))]
    for n in counts:
        sems += [dma(n), dma(n)]
    div, hg, dw = pl.pallas_call(
        kernel,
        name="distill",
        out_shape=(vmem((1, BLK), F32), vmem((SUB, WID), BF16), vmem((WID, COLS), BF16)),
        in_specs=[pl.BlockSpec(memory_space=pl.ANY)] * 3,
        out_specs=[pl.BlockSpec(memory_space=vmem)] * 3,
        scratch_shapes=scratch + sems,
        compiler_params=pltpu.CompilerParams(
            collective_id=0, has_side_effects=True, vmem_limit_bytes=54 * 1024 * 1024
        ),
    )(hidden, head_weight, teacher_logits)
    div, hg, dw = pl.pallas_call(
        put,
        name="put",
        out_shape=(
            jax.ShapeDtypeStruct((BLK,), F32),
            jax.ShapeDtypeStruct((SUB, WID), BF16),
            jax.ShapeDtypeStruct((WID, COLS), BF16),
        ),
        in_specs=[pl.BlockSpec(memory_space=vmem)] * 3,
        out_specs=[pl.BlockSpec(memory_space=vmem)] * 2 + [pl.BlockSpec(memory_space=pl.ANY)],
        scratch_shapes=[dma((7,))],
        compiler_params=pltpu.CompilerParams(vmem_limit_bytes=2 * 1024 * 1024),
    )(div, hg, dw)
    return div, hg, dw


def solution(mesh):
    return jax.shard_map(
        local,
        mesh=mesh,
        in_specs=(P("dp", None), P("dp", "vocab"), P("dp", "vocab")),
        out_specs=(P("dp"), P("vocab", "dp"), P("dp", "vocab")),
        check_vma=False,
    )
```

```python
import jax
import jax.numpy as jnp
from jax import lax
from jax.experimental import pallas as pl
from jax.experimental.pallas import tpu as pltpu
from jax.sharding import PartitionSpec as P

MESH = pl.DeviceIdType.MESH
F32, BF16 = jnp.float32, jnp.bfloat16
loss_scale = 256.0
LOW = -3.0e38

D, ROWS = 3584, 1024
NX, NY, NZ = 4, 4, 8
BLK = 128
SUB = BLK // NY
WID = D // 8
CHIP = 2 * WID
COLS = 4096
PART = COLS // NX
HSH = D // NY
THIN = BLK // NZ


STEPS = tuple((turn, first, 16) for turn, first in zip((3, 2, 3, 1, 2, 0, 1, 0), (0, 0, 16, 0, 16, 0, 16, 16)))
BEFORE = (None, 0, None, 1, 2, 3, 4, 6)
LAST = (5, 7)
FIRST = tuple(128 * s for s in range(8))
EARLY = 112
WIDE = 512
OFFERS = {0: 3, 2: 4, 3: 5, 4: 6, 6: 7}


def groups(value):
    return [value[:, 128 * g : 128 * g + 128] for g in range(value.shape[1] // 128)]


def fold(parts, op):
    while len(parts) > 1:
        parts = [op(parts[i], parts[i + 1]) for i in range(0, len(parts), 2)]
    return parts[0]


def row_max(part):
    return jnp.max(part.T, axis=0, keepdims=True)


def row_sum(part):
    return jnp.sum(part.T, axis=0, keepdims=True)


def kernel(
    h_ref, w_ref, t_ref,
    div_ref, hg_ref, dw_ref,
    hc, wc, tc, student, town, wown, wt, hx, ht, gbuf, acc,
    hgp, hgy, hgz, sx, sy, sz, last, col, cross, cx, cy, cz,
    lsem, hxs, hxr, hzs, hzr, hys, hyr, wxs, wxr, wcs, wcr, ts, tr, hcs, hcr,
    sxs, sxr, sys_, syr, szs, szr, gas, gar, gfs, gfr, gcs, gcr,
    hgys, hgyr, hgzs, hgzr, cxs, cxr, cys, cyr, czs, czr,
):
    dp, v = lax.axis_index("dp"), lax.axis_index("vocab")
    x, c = dp // 2, dp % 2
    z, y = v // NY, v % NY

    def at_x(o):
        return (lax.rem(x + o, NX) * 2 + c, v)

    def at_y(o):
        return (dp, z * NY + lax.rem(y + o, NY))

    def at_z(o):
        return (dp, lax.rem(z + o, NZ) * NY + y)

    other = (x * 2 + 1 - c, v)

    def remote(src, dst, ss, rs, device):
        return pltpu.make_async_remote_copy(
            src_ref=src, dst_ref=dst, send_sem=ss, recv_sem=rs, device_id=device, device_id_type=MESH
        )

    barrier = pltpu.get_barrier_semaphore()
    partners = [at_x(o) for o in range(1, NX)] + [other]
    partners += [at_y(o) for o in range(1, NY)] + [at_z(o) for o in range(1, NZ)]
    for p in partners:
        pl.semaphore_signal(barrier, inc=1, device_id=p, device_id_type=MESH)

    def cols_of(i):
        return pl.ds(pl.multiple_of(i * PART, PART), PART)

    def wrows(i, j):
        return pl.ds(pl.multiple_of(i * CHIP + j * WID, 64), WID)

    own_w = pltpu.make_async_copy(w_ref.at[:, cols_of(x)], wc.at[wrows(x, c)], lsem.at[0])
    share = pl.ds(pl.multiple_of(y * HSH, HSH), HSH)
    thin = [pl.ds(pl.multiple_of(lax.rem(z + NZ - o, NZ) * THIN, THIN), THIN) for o in range(NZ)]
    own_h = pltpu.make_async_copy(h_ref.at[thin[0], share], hc.at[x, thin[0], share], lsem.at[1])
    own_t = pltpu.make_async_copy(t_ref.at[:, cols_of(x)], tc.at[x], lsem.at[2])
    all_t = pltpu.make_async_copy(t_ref, town, lsem.at[3])
    all_w = pltpu.make_async_copy(w_ref, wown.at[pl.ds(0, WID)], lsem.at[4])
    for cp in (own_h, all_t, all_w, own_w, own_t):
        cp.start()
    pl.semaphore_wait(barrier, len(partners))

    h_x = [
        remote(
            h_ref.at[thin[0], share], hc.at[x, thin[0], share], hxs.at[o - 1], hxr.at[o - 1], at_x(o)
        )
        for o in range(1, NX)
    ]
    w_x = [
        remote(
            w_ref.at[:, cols_of(lax.rem(x + o, NX))], wc.at[wrows(x, c)], wxs.at[o - 1], wxr.at[o - 1], at_x(o)
        )
        for o in range(1, NX)
    ]
    t_x = [
        [
            remote(
                t_ref.at[rows, cols_of(lax.rem(x + o, NX))], tc.at[x, rows], ts.at[i, o - 1], tr.at[i, o - 1], at_x(o)
            )
            for o in range(1, NX)
        ]
        for i, rows in enumerate((pl.ds(0, EARLY), pl.ds(EARLY, BLK - EARLY)))
    ]

    def w_core(o):
        rows = wrows(lax.rem(x + NX - o, NX), c)
        src = w_ref.at[:, cols_of(x)] if o == 0 else wc.at[rows]
        return remote(src, wc.at[rows], wcs.at[o], wcr.at[o], other)

    w_c = [w_core(o) for o in range(NX)]
    for cp in h_x + w_x:
        cp.start()
    w_c[0].start()

    own_h.wait()
    for cp in h_x:
        cp.wait_recv()
    shares = [hc.at[:, rows, share] for rows in thin]
    h_z = [remote(shares[0], shares[0], hzs.at[o - 1], hzr.at[o - 1], at_z(o)) for o in range(1, NZ)]
    h_y = [
        [remote(part, part, hys.at[i, o - 1], hyr.at[i, o - 1], at_y(o)) for o in range(1, NY)]
        for i, part in enumerate(shares)
    ]
    nearest = (1, 7, 2, 6, 3, 5, 4)
    for cp in [h_z[o - 1] for o in nearest] + h_y[0]:
        cp.start()

    for b in range(NX):
        sy[y, b] = jnp.where(lax.broadcasted_iota(jnp.int32, (8, BLK), 0) % 2 == 0, LOW, 0.0)
    all_t.wait()
    part = fold([town[:, 128 * g : 128 * g + 128] for g in range(COLS // 128)], jnp.maximum)
    top = jnp.max(part, axis=1, keepdims=True)
    total = fold([jnp.exp(town[:, 128 * g : 128 * g + 128] - top) for g in range(COLS // 128)], jnp.add)
    sy[y, x, 2:3, :] = row_max(part)
    sy[y, x, 3:4, :] = row_sum(total)

    all_w.wait()
    wown[WID:] = jnp.zeros((WIDE - WID, COLS), BF16)

    def turn(i, carry):
        cols = pl.ds(pl.multiple_of(i * 512, 512), 512)
        wt[cols, :] = wown[:, cols].T
        return carry

    lax.fori_loop(0, COLS // 512, turn, 0)

    for o in nearest:
        h_z[o - 1].wait_recv()
        for cp in h_y[o]:
            cp.start()
    for o in (1, 3, 2):
        w_x[o - 1].wait_recv()
        w_c[o].start()
    for cp in w_x:
        cp.wait_send()
    for cp in t_x[0]:
        cp.start()
    for cp in sum(h_y, []):
        cp.wait_recv()

    mine = pl.ds(pl.multiple_of(x * CHIP, CHIP), CHIP)
    h_c = remote(hc.at[:, :, mine], hx.at[c], hcs.at[0], hcr.at[0], other)
    h_c.start()
    keep = pltpu.make_async_copy(hc.at[:, :, mine], hx.at[c], lsem.at[5])
    keep.start()
    own_w.wait()
    for cp in w_c:
        cp.wait_recv()

    def score(i, carry):
        cols = pl.ds(pl.multiple_of(i * 256, 256), 256)
        tile = jnp.dot(hc[...].reshape(NX * BLK, D), wc[:, cols], preferred_element_type=F32)
        student[:, :, cols] = tile.reshape(NX, BLK, 256)
        return carry

    lax.fori_loop(0, PART // 256, score, 0)

    def local_stats(b, carry):
        parts = groups(student[b])
        part = fold(parts, jnp.maximum)
        top = jnp.max(part, axis=1, keepdims=True)
        total = fold([jnp.exp(p - top) for p in parts], jnp.add)
        sy[y, b, 0:1, :] = row_max(part)
        sy[y, b, 1:2, :] = row_sum(total)
        return carry

    lax.fori_loop(0, NX, local_stats, 0)

    def reduce_stats(slots, count, target):
        for b in range(NX):
            m_s = fold([slots[i, b, 0:1, :] for i in range(count)], jnp.maximum)
            m_t = fold([slots[i, b, 2:3, :] for i in range(count)], jnp.maximum)
            l_s = fold([slots[i, b, 1:2, :] * jnp.exp(slots[i, b, 0:1, :] - m_s) for i in range(count)], jnp.add)
            l_t = fold([slots[i, b, 3:4, :] * jnp.exp(slots[i, b, 2:3, :] - m_t) for i in range(count)], jnp.add)
            target(b, m_s, l_s, m_t, l_t)

    def into(slots, me):
        def put(b, *values):
            for r, value in enumerate(values):
                slots[me, b, r : r + 1, :] = value

        return put

    s_x = [remote(sx.at[x], sx.at[x], sxs.at[o - 1], sxr.at[o - 1], at_x(o)) for o in range(1, NX)]
    s_y = [remote(sy.at[y], sy.at[y], sys_.at[o - 1], syr.at[o - 1], at_y(o)) for o in range(1, NY)]
    s_z = [remote(sz.at[z], sz.at[z], szs.at[o - 1], szr.at[o - 1], at_z(o)) for o in range(1, NZ)]
    for cp in s_y:
        cp.start()
    for cp in s_y:
        cp.wait_recv()
    reduce_stats(sy, NY, into(sz, z))
    for cp in s_z:
        cp.start()
    for cp in s_z:
        cp.wait_recv()
    reduce_stats(sz, NZ, into(sx, x))
    for cp in s_x + t_x[1]:
        cp.start()
    for cp in s_x:
        cp.wait_recv()
    def columns(b, m_s, l_s, m_t, l_t):
        for r, value in enumerate((m_s, loss_scale / l_s, m_t, loss_scale / l_t)):
            col[r, b] = jnp.broadcast_to(value, (BLK, BLK)).T
        last[b, 0:1, :] = m_s + jnp.log(l_s) - m_t - jnp.log(l_t)
        last[b, 1:2, :] = l_t

    reduce_stats(sx, NX, columns)

    own_t.wait()
    for cp in t_x[0] + t_x[1]:
        cp.wait_recv()

    def rows_at(s, plane):
        turn = STEPS[s][0]
        k = lax.rem(y + turn, NY) if plane == 0 else lax.rem(y + NY - turn, NY)
        return pl.ds(pl.multiple_of(k * SUB + STEPS[s][1], 16), STEPS[s][2])

    def rows_mine(s):
        turn = STEPS[s][0]
        k = lax.rem(y + turn + c * (2 * NY - 2 * turn), NY)
        return pl.ds(pl.multiple_of(k * SUB + STEPS[s][1], 16), STEPS[s][2])

    def piece(s, owner, part, parts):
        size = NX * STEPS[s][2]
        first = FIRST[s] + c * size + part * (size // parts)
        return gbuf.at[pl.ds(pl.multiple_of(first, 32), size // parts), cols_of(owner)]

    left, right, far = lax.rem(x + 3, NX), lax.rem(x + 1, NX), lax.rem(x + 2, NX)
    owners = [x, left, far, right]
    g_a, g_f, g_c = [], [], []
    for s in range(len(STEPS)):
        own, low, high = piece(s, x, 0, 1), piece(s, left, 0, 2), piece(s, right, 1, 2)
        g_a.append([remote(own, own, gas.at[s, i], gar.at[s, i], at_x(o)) for i, o in enumerate((1, 3))])
        g_f.append(
            [
                remote(low, low, gfs.at[s, 0], gfr.at[s, 0], at_x(1)),
                remote(high, high, gfs.at[s, 1], gfr.at[s, 1], at_x(3)),
            ]
        )
        blocks = [piece(s, q, 0, 1) for q in owners]
        g_c.append([remote(q, q, gcs.at[s, o], gcr.at[s, o], other) for o, q in enumerate(blocks)])

    def make(s):
        rows, count = rows_mine(s), STEPS[s][2]

        def grad(b, carry):
            m_s, a_s, m_t, a_t = [col[r, b, rows, :] for r in range(4)]
            out = pl.ds(pl.multiple_of(FIRST[s] + c * (NX * count) + b * count, 16), count)
            total = jnp.zeros((count, 128), F32)
            tiles = []
            for g in range(PART // 128):
                st = student[b, rows, 128 * g : 128 * g + 128]
                te = tc[b, rows, 128 * g : 128 * g + 128]
                e_t = jnp.exp(te - m_t)
                total += e_t * (te - st)
                tiles.append((jnp.exp(st - m_s) * a_s - e_t * a_t).astype(BF16))
            gbuf[out, cols_of(x)] = jnp.concatenate(tiles, axis=1)
            cross[b, rows, :] = total
            return carry

        lax.fori_loop(0, NX, grad, 0)

    def offer(s):
        for cp in g_a[s]:
            cp.start()
        g_c[s][0].start()

    def pass_on(s):
        for i, o in enumerate((1, 3)):
            g_a[s][i].wait_recv()
            g_f[s][i].start()
            g_c[s][o].start()

    make(0)
    offer(0)
    for s in range(1, len(STEPS)):
        make(s)
    for b in range(NX):
        cx[x, b] = jnp.broadcast_to(row_sum(cross[b]), (8, BLK))
    offer(1)

    keep.wait()
    h_c.wait_recv()
    for s in range(len(STEPS)):
        if s == 4:
            offer(2)
        count = STEPS[s][2]
        block = jnp.concatenate([hx[j, b, rows_at(s, j), :] for j in range(2) for b in range(NX)], axis=0)
        block = pltpu.roll(block.astype(F32), lax.rem(c * WID, CHIP), 1)[:, :512]
        ht[:, FIRST[s] : FIRST[s] + 2 * NX * count] = block.T[:WID].astype(BF16)

    c_x = [
        remote(
            cx.at[x, lax.rem(x + o, NX)], cx.at[x, lax.rem(x + o, NX)], cxs.at[o - 1], cxr.at[o - 1], at_x(o)
        )
        for o in range(1, NX)
    ]
    c_y = [remote(cy.at[y], cy.at[y], cys.at[o - 1], cyr.at[o - 1], at_y(o)) for o in range(1, NY)]
    c_z = [remote(cz.at[z], cz.at[z], czs.at[o - 1], czr.at[o - 1], at_z(o)) for o in range(1, NZ)]

    def to_y(s, j):
        rows = pl.ds(s * BLK + j * 64, 64)
        return remote(hgp.at[rows], hgy.at[rows], hgys.at[s, j], hgyr.at[s, j], at_y(NY - 1 if j else 1))

    def to_z(i, o):
        zz = lax.rem(z + o, NZ)
        rows = pl.ds(pl.multiple_of(LAST[i] * BLK + (zz % 2) * 64 + (zz // 2) * 16, 16), 16)
        return remote(hgp.at[rows], hgz.at[o - 1, pl.ds(16 * i, 16)], hgzs.at[i, o - 1], hgzr.at[i, o - 1], at_z(o))

    h_to_y = [[to_y(s, j) for j in range(2)] if STEPS[s][0] else [] for s in range(len(STEPS))]
    h_to_z = [[to_z(i, o) for o in range(1, NZ)] for i in range(2)]

    def far_in(s):
        for cp in g_f[s]:
            cp.wait_recv()
        g_c[s][2].start()

    def product(s):
        for cp in g_c[s]:
            cp.wait_recv()
        rows = slice(FIRST[s], FIRST[s] + BLK)
        hgp[rows] = jnp.dot(gbuf[rows], wt[...], preferred_element_type=F32)
        if BEFORE[s] is not None:
            for cp in h_to_y[BEFORE[s]]:
                cp.wait_recv()
            hgp[rows] += hgy[FIRST[BEFORE[s]] : FIRST[BEFORE[s]] + BLK]
        for cp in h_to_y[s] or h_to_z[LAST.index(s)]:
            cp.start()

    def head_product(i, first, last):
        depth = slice(512 * i, 512 * i + 512)

        def head(n, carry):
            cols = pl.ds(pl.multiple_of(n * 512, 512), 512)
            tile = jnp.dot(ht[:, depth], gbuf[depth, cols], preferred_element_type=F32)
            if i == 0:
                acc[:, cols] = tile
            else:
                dw_ref[:, cols] = (acc[:, cols] + tile).astype(BF16)
            return carry

        lax.fori_loop(first, last, head, 0)

    def near(s):
        pass_on(s)
        if s in OFFERS:
            offer(OFFERS[s])

    near(0)
    near(1)
    for cp in c_x:
        cp.start()
    near(2)
    far_in(0)
    product(0)
    far_in(1)
    near(3)
    far_in(2)
    product(1)
    for cp in c_x:
        cp.wait_recv()
    cy[y] = cx[0, x] + cx[1, x] + cx[2, x] + cx[3, x]
    for cp in c_y:
        cp.start()
    near(4)
    product(2)
    far_in(3)
    product(3)
    head_product(0, 0, 2)
    far_in(4)
    near(5)
    near(6)
    for cp in c_y:
        cp.wait_recv()
    cz[z] = cy[0] + cy[1] + cy[2] + cy[3]
    for cp in c_z:
        cp.start()
    product(4)
    far_in(5)
    head_product(0, 2, 4)
    product(5)
    far_in(6)
    near(7)
    product(6)
    head_product(0, 4, 6)
    far_in(7)
    product(7)
    head_product(0, 6, 8)
    head_product(1, 0, 8)

    for cp in c_z:
        cp.wait_recv()
    crossed = fold([cz[i, 0:1, :] for i in range(NZ)], jnp.add)
    div_ref[...] = crossed / last[x, 1:2, :] + last[x, 0:1, :]

    for i in range(2):
        for cp in h_to_z[i]:
            cp.wait_recv()
        mine = pl.ds(pl.multiple_of(LAST[i] * BLK + (z % 2) * 64 + (z // 2) * 16, 16), 16)
        total = hgp[mine, :]
        for o in range(NZ - 1):
            total = total + hgz[o, 16 * i : 16 * i + 16]
        hg_ref[16 * i : 16 * i + 16, :] = total[:, :WID].astype(BF16)

    sent = h_x + h_z + [h_c] + w_c + s_x + s_y + s_z + c_x + c_y + c_z
    for cp in sent + sum(h_y + t_x + g_a + g_f + g_c + h_to_y + h_to_z, []):
        cp.wait_send()


def put(div_in, hg_in, dw_in, div_ref, hg_ref, dw_ref, sems):
    rows = WID // 7
    parts = [pl.ds(rows * i, rows) for i in range(7)]
    copies = [pltpu.make_async_copy(dw_in.at[p], dw_ref.at[p], sems.at[i]) for i, p in enumerate(parts)]
    for cp in copies:
        cp.start()
    div_ref[...] = div_in[0]
    hg_ref[...] = hg_in[...]
    for cp in copies:
        cp.wait()


def local(hidden, head_weight, teacher_logits):
    dma = pltpu.SemaphoreType.DMA
    vmem = pltpu.VMEM
    scratch = [
        vmem((NX, BLK, D), BF16),
        vmem((D, PART), BF16),
        vmem((NX, BLK, PART), F32),
        vmem((NX, BLK, PART), F32),
        vmem((BLK, COLS), F32),
        vmem((WIDE, COLS), BF16),
        vmem((COLS, WIDE), BF16),
        vmem((2, NX, BLK, CHIP), BF16),
        vmem((WID, ROWS), BF16),
        vmem((ROWS, COLS), BF16),
        vmem((WID, COLS), F32),
        vmem((ROWS, WIDE), F32),
        vmem((ROWS, WIDE), F32),
        vmem((NZ - 1, SUB, WIDE), F32),
        vmem((NX, NX, 8, BLK), F32),
        vmem((NY, NX, 8, BLK), F32),
        vmem((NZ, NX, 8, BLK), F32),
        vmem((NX, 8, BLK), F32),
        vmem((4, NX, BLK, BLK), F32),
        vmem((NX, BLK, BLK), F32),
        vmem((NX, NX, 8, BLK), F32),
        vmem((NY, 8, BLK), F32),
        vmem((NZ, 8, BLK), F32),
    ]
    counts = [(3,), (7,), (8, 3), (3,), (4,), (2, 3), (1,), (3,), (3,), (7,)]
    counts += [(8, 2), (8, 2), (8, 4), (8, 2), (2, 7), (3,), (3,), (7,)]
    sems = [dma((6,))]
    for n in counts:
        sems += [dma(n), dma(n)]
    div, hg, dw = pl.pallas_call(
        kernel,
        name="distill",
        out_shape=(vmem((1, BLK), F32), vmem((SUB, WID), BF16), vmem((WID, COLS), BF16)),
        in_specs=[pl.BlockSpec(memory_space=pl.ANY)] * 3,
        out_specs=[pl.BlockSpec(memory_space=vmem)] * 3,
        scratch_shapes=scratch + sems,
        compiler_params=pltpu.CompilerParams(
            collective_id=0, has_side_effects=True, vmem_limit_bytes=54 * 1024 * 1024
        ),
    )(hidden, head_weight, teacher_logits)
    div, hg, dw = pl.pallas_call(
        put,
        name="put",
        out_shape=(
            jax.ShapeDtypeStruct((BLK,), F32),
            jax.ShapeDtypeStruct((SUB, WID), BF16),
            jax.ShapeDtypeStruct((WID, COLS), BF16),
        ),
        in_specs=[pl.BlockSpec(memory_space=vmem)] * 3,
        out_specs=[pl.BlockSpec(memory_space=vmem)] * 2 + [pl.BlockSpec(memory_space=pl.ANY)],
        scratch_shapes=[dma((7,))],
        compiler_params=pltpu.CompilerParams(vmem_limit_bytes=2 * 1024 * 1024),
    )(div, hg, dw)
    return div, hg, dw


def solution(mesh):
    return jax.shard_map(
        local,
        mesh=mesh,
        in_specs=(P("dp", None), P("dp", "vocab"), P("dp", "vocab")),
        out_specs=(P("dp"), P("vocab", "dp"), P("dp", "vocab")),
        check_vma=False,
    )
```

```python
import jax
import jax.numpy as jnp
from jax import lax
from jax.experimental import pallas as pl
from jax.experimental.pallas import tpu as pltpu
from jax.sharding import PartitionSpec as P

MESH = pl.DeviceIdType.MESH
F32, BF16 = jnp.float32, jnp.bfloat16
loss_scale = 256.0
LOW = -3.0e38

D, ROWS = 3584, 1024
NX, NY, NZ = 4, 4, 8
BLK = 128
SUB = BLK // NY
WID = D // 8
CHIP = 2 * WID
COLS = 4096
PART = COLS // NX
HSH = D // NY
THIN = BLK // NZ


STEPS = tuple((turn, first, 16) for turn, first in zip((3, 2, 3, 1, 2, 0, 1, 0), (0, 0, 16, 0, 16, 0, 16, 16)))
BEFORE = (None, 0, None, 1, 2, 3, 4, 6)
LAST = (5, 7)
FIRST = tuple(128 * s for s in range(8))
OFFERS = {0: 3, 2: 4, 3: 5, 4: 6, 6: 7}
EARLY = 112
WIDE = 512


def groups(value):
    return [value[:, 128 * g : 128 * g + 128] for g in range(value.shape[1] // 128)]


def fold(parts, op):
    while len(parts) > 1:
        parts = [op(parts[i], parts[i + 1]) for i in range(0, len(parts), 2)]
    return parts[0]


def row_max(part):
    return jnp.max(part.T, axis=0, keepdims=True)


def row_sum(part):
    return jnp.sum(part.T, axis=0, keepdims=True)


def kernel(
    h_ref, w_ref, t_ref,
    div_ref, hg_ref, dw_ref,
    hc, wc, tc, student, town, wown, wt, hx, ht, gbuf, acc,
    hgp, hgy, hgz, sx, sy, sz, last, col, cross, cx, cy, cz,
    lsem, own_s, own_r, two_s, two_r, wcs, wcr, ts, tr, hcs, hcr, sxs, sxr,
    gfs, gfr, hgys, hgyr, hgzs, hgzr, cxs, cxr, cys, cyr, czs, czr,
):
    dp, v = lax.axis_index("dp"), lax.axis_index("vocab")
    x, c = dp // 2, dp % 2
    z, y = v // NY, v % NY

    def at_x(o):
        return (lax.rem(x + o, NX) * 2 + c, v)

    def at_y(o):
        return (dp, z * NY + lax.rem(y + o, NY))

    def at_z(o):
        return (dp, lax.rem(z + o, NZ) * NY + y)

    other = (x * 2 + 1 - c, v)

    def remote(src, dst, ss, rs, device):
        return pltpu.make_async_remote_copy(
            src_ref=src, dst_ref=dst, send_sem=ss, recv_sem=rs, device_id=device, device_id_type=MESH
        )

    barrier = pltpu.get_barrier_semaphore()
    partners = [at_x(o) for o in range(1, NX)] + [other]
    partners += [at_y(o) for o in range(1, NY)] + [at_z(o) for o in range(1, NZ)]
    for p in partners:
        pl.semaphore_signal(barrier, inc=1, device_id=p, device_id_type=MESH)

    def cols_of(i):
        return pl.ds(pl.multiple_of(i * PART, PART), PART)

    def wrows(i, j):
        return pl.ds(pl.multiple_of(i * CHIP + j * WID, 64), WID)

    own_w = pltpu.make_async_copy(w_ref.at[:, cols_of(x)], wc.at[wrows(x, c)], lsem.at[0])
    share = pl.ds(pl.multiple_of(y * HSH, HSH), HSH)
    thin = [pl.ds(pl.multiple_of(lax.rem(z + NZ - o, NZ) * THIN, THIN), THIN) for o in range(NZ)]
    own_h = pltpu.make_async_copy(h_ref.at[thin[0], share], hc.at[x, thin[0], share], lsem.at[1])
    own_t = pltpu.make_async_copy(t_ref.at[:, cols_of(x)], tc.at[x], lsem.at[2])
    all_t = pltpu.make_async_copy(t_ref, town, lsem.at[3])
    all_w = pltpu.make_async_copy(w_ref, wown.at[pl.ds(0, WID)], lsem.at[4])
    for cp in (own_h, all_t, all_w, own_w, own_t):
        cp.start()
    pl.semaphore_wait(barrier, len(partners))

    h_x = [
        remote(
            h_ref.at[thin[0], share], hc.at[x, thin[0], share], own_s.at[o - 1], own_r.at[o - 1], at_x(o)
        )
        for o in range(1, NX)
    ]
    w_x = [
        remote(
            w_ref.at[:, cols_of(lax.rem(x + o, NX))], wc.at[wrows(x, c)], own_s.at[o + 2], own_r.at[o + 2], at_x(o)
        )
        for o in range(1, NX)
    ]
    t_x = [
        [
            remote(
                t_ref.at[rows, cols_of(lax.rem(x + o, NX))], tc.at[x, rows], ts.at[i, o - 1], tr.at[i, o - 1], at_x(o)
            )
            for o in range(1, NX)
        ]
        for i, rows in enumerate((pl.ds(0, EARLY), pl.ds(EARLY, BLK - EARLY)))
    ]

    def w_core(o):
        rows = wrows(lax.rem(x + NX - o, NX), c)
        src = w_ref.at[:, cols_of(x)] if o == 0 else wc.at[rows]
        return remote(src, wc.at[rows], wcs.at[o], wcr.at[o], other)

    w_c = [w_core(o) for o in range(NX)]
    for cp in h_x + w_x:
        cp.start()
    w_c[0].start()

    own_h.wait()
    for cp in h_x:
        cp.wait_recv()
    shares = [hc.at[:, rows, share] for rows in thin]
    h_z = [remote(shares[0], shares[0], two_s.at[o - 1, 3], two_r.at[o - 1, 3], at_z(o)) for o in range(1, NZ)]
    h_y = [
        [remote(part, part, two_s.at[i, o - 1], two_r.at[i, o - 1], at_y(o)) for o in range(1, NY)]
        for i, part in enumerate(shares)
    ]
    nearest = (1, 7, 2, 6, 3, 5, 4)
    for cp in [h_z[o - 1] for o in nearest] + h_y[0]:
        cp.start()

    for b in range(NX):
        sy[y, b] = jnp.where(lax.broadcasted_iota(jnp.int32, (8, BLK), 0) % 2 == 0, LOW, 0.0)
    all_t.wait()
    part = fold([town[:, 128 * g : 128 * g + 128] for g in range(COLS // 128)], jnp.maximum)
    top = jnp.max(part, axis=1, keepdims=True)
    total = fold([jnp.exp(town[:, 128 * g : 128 * g + 128] - top) for g in range(COLS // 128)], jnp.add)
    sy[y, x, 2:3, :] = row_max(part)
    sy[y, x, 3:4, :] = row_sum(total)

    all_w.wait()
    wown[WID:] = jnp.zeros((WIDE - WID, COLS), BF16)

    def turn(i, carry):
        cols = pl.ds(pl.multiple_of(i * 512, 512), 512)
        wt[cols, :] = wown[:, cols].T
        return carry

    lax.fori_loop(0, COLS // 512, turn, 0)

    for o in nearest:
        h_z[o - 1].wait_recv()
        for cp in h_y[o]:
            cp.start()
    for o in (1, 3, 2):
        w_x[o - 1].wait_recv()
        w_c[o].start()
    for cp in t_x[0]:
        cp.start()
    for cp in sum(h_y, []):
        cp.wait_recv()

    mine = pl.ds(pl.multiple_of(x * CHIP, CHIP), CHIP)
    h_c = remote(hc.at[:, :, mine], hx.at[c], hcs.at[0], hcr.at[0], other)
    h_c.start()
    keep = pltpu.make_async_copy(hc.at[:, :, mine], hx.at[c], lsem.at[5])
    keep.start()
    own_w.wait()
    for cp in w_c:
        cp.wait_recv()

    def score(i, carry):
        cols = pl.ds(pl.multiple_of(i * 256, 256), 256)
        tile = jnp.dot(hc[...].reshape(NX * BLK, D), wc[:, cols], preferred_element_type=F32)
        student[:, :, cols] = tile.reshape(NX, BLK, 256)
        return carry

    lax.fori_loop(0, PART // 256, score, 0)

    def local_stats(b, carry):
        parts = groups(student[b])
        part = fold(parts, jnp.maximum)
        top = jnp.max(part, axis=1, keepdims=True)
        total = fold([jnp.exp(p - top) for p in parts], jnp.add)
        sy[y, b, 0:1, :] = row_max(part)
        sy[y, b, 1:2, :] = row_sum(total)
        return carry

    lax.fori_loop(0, NX, local_stats, 0)

    def reduce_stats(slots, count, target):
        for b in range(NX):
            m_s = fold([slots[i, b, 0:1, :] for i in range(count)], jnp.maximum)
            m_t = fold([slots[i, b, 2:3, :] for i in range(count)], jnp.maximum)
            l_s = fold([slots[i, b, 1:2, :] * jnp.exp(slots[i, b, 0:1, :] - m_s) for i in range(count)], jnp.add)
            l_t = fold([slots[i, b, 3:4, :] * jnp.exp(slots[i, b, 2:3, :] - m_t) for i in range(count)], jnp.add)
            target(b, m_s, l_s, m_t, l_t)

    def into(slots, me):
        def put(b, *values):
            for r, value in enumerate(values):
                slots[me, b, r : r + 1, :] = value

        return put

    s_x = [remote(sx.at[x], sx.at[x], sxs.at[o - 1], sxr.at[o - 1], at_x(o)) for o in range(1, NX)]
    s_y = [remote(sy.at[y], sy.at[y], own_s.at[o + 5], own_r.at[o + 5], at_y(o)) for o in range(1, NY)]
    s_z = [remote(sz.at[z], sz.at[z], own_s.at[o + 8], own_r.at[o + 8], at_z(o)) for o in range(1, NZ)]
    for cp in s_y:
        cp.start()
    for cp in s_y:
        cp.wait_recv()
    reduce_stats(sy, NY, into(sz, z))
    for cp in s_z:
        cp.start()
    for cp in s_z:
        cp.wait_recv()
    reduce_stats(sz, NZ, into(sx, x))
    for cp in s_x + t_x[1]:
        cp.start()
    for cp in s_x:
        cp.wait_recv()
    def columns(b, m_s, l_s, m_t, l_t):
        for r, value in enumerate((m_s, loss_scale / l_s, m_t, loss_scale / l_t)):
            col[r, b] = jnp.broadcast_to(value, (BLK, BLK)).T
        last[b, 0:1, :] = m_s + jnp.log(l_s) - m_t - jnp.log(l_t)
        last[b, 1:2, :] = l_t

    reduce_stats(sx, NX, columns)

    keep.wait()
    h_c.wait_recv()
    for cp in h_x + w_x + h_z + sum(h_y, []) + s_x + s_y + s_z:
        cp.wait_send()
    own_t.wait()
    for cp in t_x[0] + t_x[1]:
        cp.wait_recv()

    def rows_at(s, plane):
        turn = STEPS[s][0]
        k = lax.rem(y + turn, NY) if plane == 0 else lax.rem(y + NY - turn, NY)
        return pl.ds(pl.multiple_of(k * SUB + STEPS[s][1], 16), STEPS[s][2])

    def rows_mine(s):
        turn = STEPS[s][0]
        k = lax.rem(y + turn + c * (2 * NY - 2 * turn), NY)
        return pl.ds(pl.multiple_of(k * SUB + STEPS[s][1], 16), STEPS[s][2])

    def piece(s, owner, part, parts):
        size = NX * STEPS[s][2]
        first = FIRST[s] + c * size + part * (size // parts)
        return gbuf.at[pl.ds(pl.multiple_of(first, 32), size // parts), cols_of(owner)]

    left, right, far = lax.rem(x + 3, NX), lax.rem(x + 1, NX), lax.rem(x + 2, NX)
    owners = [x, left, far, right]
    g_a, g_f, g_c = [], [], []
    for s in range(len(STEPS)):
        own, low, high = piece(s, x, 0, 1), piece(s, left, 0, 2), piece(s, right, 1, 2)
        g_a.append([remote(own, own, own_s.at[2 * s + i], own_r.at[2 * s + i], at_x(o)) for i, o in enumerate((1, 3))])
        g_f.append(
            [
                remote(low, low, gfs.at[s, 0], gfr.at[s, 0], at_x(1)),
                remote(high, high, gfs.at[s, 1], gfr.at[s, 1], at_x(3)),
            ]
        )
        blocks = [piece(s, q, 0, 1) for q in owners]
        g_c.append([remote(q, q, two_s.at[s, o], two_r.at[s, o], other) for o, q in enumerate(blocks)])

    def make(s):
        rows, count = rows_mine(s), STEPS[s][2]

        def grad(b, carry):
            m_s, a_s, m_t, a_t = [col[r, b, rows, :] for r in range(4)]
            out = pl.ds(pl.multiple_of(FIRST[s] + c * (NX * count) + b * count, 16), count)
            total = jnp.zeros((count, 128), F32)
            tiles = []
            for g in range(PART // 128):
                st = student[b, rows, 128 * g : 128 * g + 128]
                te = tc[b, rows, 128 * g : 128 * g + 128]
                e_t = jnp.exp(te - m_t)
                total += e_t * (te - st)
                tiles.append((jnp.exp(st - m_s) * a_s - e_t * a_t).astype(BF16))
            gbuf[out, cols_of(x)] = jnp.concatenate(tiles, axis=1)
            cross[b, rows, :] = total
            return carry

        lax.fori_loop(0, NX, grad, 0)

    def offer(s):
        for cp in g_a[s]:
            cp.start()
        g_c[s][0].start()

    def pass_on(s):
        for i, o in enumerate((1, 3)):
            g_a[s][i].wait_recv()
            g_f[s][i].start()
            g_c[s][o].start()

    make(0)
    offer(0)
    for s in range(1, len(STEPS)):
        make(s)
    for b in range(NX):
        cx[x, b] = jnp.broadcast_to(row_sum(cross[b]), (8, BLK))
    offer(1)

    for s in range(len(STEPS)):
        if s == 4:
            offer(2)
        count = STEPS[s][2]
        block = jnp.concatenate([hx[j, b, rows_at(s, j), :] for j in range(2) for b in range(NX)], axis=0)
        block = pltpu.roll(block.astype(F32), lax.rem(c * WID, CHIP), 1)[:, :512]
        ht[:, FIRST[s] : FIRST[s] + 2 * NX * count] = block.T[:WID].astype(BF16)

    c_x = [
        remote(
            cx.at[x, lax.rem(x + o, NX)], cx.at[x, lax.rem(x + o, NX)], cxs.at[o - 1], cxr.at[o - 1], at_x(o)
        )
        for o in range(1, NX)
    ]
    c_y = [remote(cy.at[y], cy.at[y], cys.at[o - 1], cyr.at[o - 1], at_y(o)) for o in range(1, NY)]
    c_z = [remote(cz.at[z], cz.at[z], czs.at[o - 1], czr.at[o - 1], at_z(o)) for o in range(1, NZ)]

    def to_y(s, j):
        rows = pl.ds(s * BLK + j * 64, 64)
        return remote(hgp.at[rows], hgy.at[rows], hgys.at[s, j], hgyr.at[s, j], at_y(NY - 1 if j else 1))

    def to_z(i, o):
        zz = lax.rem(z + o, NZ)
        rows = pl.ds(pl.multiple_of(LAST[i] * BLK + (zz % 2) * 64 + (zz // 2) * 16, 16), 16)
        return remote(hgp.at[rows], hgz.at[o - 1, pl.ds(16 * i, 16)], hgzs.at[i, o - 1], hgzr.at[i, o - 1], at_z(o))

    h_to_y = [[to_y(s, j) for j in range(2)] if STEPS[s][0] else [] for s in range(len(STEPS))]
    h_to_z = [[to_z(i, o) for o in range(1, NZ)] for i in range(2)]

    def far_in(s):
        for cp in g_f[s]:
            cp.wait_recv()
        g_c[s][2].start()

    def product(s):
        for cp in g_c[s]:
            cp.wait_recv()
        rows = slice(FIRST[s], FIRST[s] + BLK)
        hgp[rows] = jnp.dot(gbuf[rows], wt[...], preferred_element_type=F32)
        if BEFORE[s] is not None:
            for cp in h_to_y[BEFORE[s]]:
                cp.wait_recv()
            hgp[rows] += hgy[FIRST[BEFORE[s]] : FIRST[BEFORE[s]] + BLK]
        for cp in h_to_y[s] or h_to_z[LAST.index(s)]:
            cp.start()

    def head_product(i, first, last):
        depth = slice(512 * i, 512 * i + 512)

        def head(n, carry):
            cols = pl.ds(pl.multiple_of(n * 512, 512), 512)
            tile = jnp.dot(ht[:, depth], gbuf[depth, cols], preferred_element_type=F32)
            if i == 0:
                acc[:, cols] = tile
            else:
                dw_ref[:, cols] = (acc[:, cols] + tile).astype(BF16)
            return carry

        lax.fori_loop(first, last, head, 0)

    def near(s):
        pass_on(s)
        if s in OFFERS:
            offer(OFFERS[s])

    near(0)
    near(1)
    for cp in c_x:
        cp.start()
    near(2)
    far_in(0)
    product(0)
    far_in(1)
    near(3)
    far_in(2)
    product(1)
    for cp in c_x:
        cp.wait_recv()
    cy[y] = cx[0, x] + cx[1, x] + cx[2, x] + cx[3, x]
    for cp in c_y:
        cp.start()
    near(4)
    product(2)
    far_in(3)
    product(3)
    head_product(0, 0, 2)
    far_in(4)
    near(5)
    near(6)
    for cp in c_y:
        cp.wait_recv()
    cz[z] = cy[0] + cy[1] + cy[2] + cy[3]
    for cp in c_z:
        cp.start()
    product(4)
    far_in(5)
    head_product(0, 2, 4)
    product(5)
    far_in(6)
    near(7)
    product(6)
    head_product(0, 4, 6)
    far_in(7)
    product(7)
    head_product(0, 6, 8)
    head_product(1, 0, 8)

    for cp in c_z:
        cp.wait_recv()
    crossed = fold([cz[i, 0:1, :] for i in range(NZ)], jnp.add)
    div_ref[...] = (crossed / last[x, 1:2, :] + last[x, 0:1, :])[0]

    for i in range(2):
        for cp in h_to_z[i]:
            cp.wait_recv()
        mine = pl.ds(pl.multiple_of(LAST[i] * BLK + (z % 2) * 64 + (z // 2) * 16, 16), 16)
        total = hgp[mine, :]
        for o in range(NZ - 1):
            total = total + hgz[o, 16 * i : 16 * i + 16]
        hg_ref[16 * i : 16 * i + 16, :] = total[:, :WID].astype(BF16)

    sent = [h_c] + w_c + c_x + c_y + c_z
    for cp in sent + sum(t_x + g_a + g_f + g_c + h_to_y + h_to_z, []):
        cp.wait_send()


def put(div_in, hg_in, dw_in, div_ref, hg_ref, dw_ref, sems):
    rows = WID // 4
    parts = [(dw_in.at[pl.ds(rows * i, rows)], dw_ref.at[pl.ds(rows * i, rows)]) for i in range(4)]
    parts += [(div_in, div_ref), (hg_in, hg_ref)]
    copies = [pltpu.make_async_copy(src, dst, sems.at[i]) for i, (src, dst) in enumerate(parts)]
    for cp in copies:
        cp.start()
    for cp in copies:
        cp.wait()


def local(hidden, head_weight, teacher_logits):
    dma = pltpu.SemaphoreType.DMA
    vmem = pltpu.VMEM
    scratch = [
        vmem((NX, BLK, D), BF16),
        vmem((D, PART), BF16),
        vmem((NX, BLK, PART), F32),
        vmem((NX, BLK, PART), F32),
        vmem((BLK, COLS), F32),
        vmem((WIDE, COLS), BF16),
        vmem((COLS, WIDE), BF16),
        vmem((2, NX, BLK, CHIP), BF16),
        vmem((WID, ROWS), BF16),
        vmem((ROWS, COLS), BF16),
        vmem((WID, COLS), F32),
        vmem((ROWS, WIDE), F32),
        vmem((ROWS, WIDE), F32),
        vmem((NZ - 1, SUB, WIDE), F32),
        vmem((NX, NX, 8, BLK), F32),
        vmem((NY, NX, 8, BLK), F32),
        vmem((NZ, NX, 8, BLK), F32),
        vmem((NX, 8, BLK), F32),
        vmem((4, NX, BLK, BLK), F32),
        vmem((NX, BLK, BLK), F32),
        vmem((NX, NX, 8, BLK), F32),
        vmem((NY, 8, BLK), F32),
        vmem((NZ, 8, BLK), F32),
    ]
    counts = [(16,), (8, 4), (4,), (2, 3), (1,), (3,), (8, 2), (8, 2), (2, 7), (3,), (3,), (7,)]
    sems = [dma((6,))]
    for n in counts:
        sems += [dma(n), dma(n)]
    div, hg, dw = pl.pallas_call(
        kernel,
        name="distill",
        out_shape=(vmem((BLK,), F32), vmem((SUB, WID), BF16), vmem((WID, COLS), BF16)),
        in_specs=[pl.BlockSpec(memory_space=pl.ANY)] * 3,
        out_specs=[pl.BlockSpec(memory_space=vmem)] * 3,
        scratch_shapes=scratch + sems,
        compiler_params=pltpu.CompilerParams(
            collective_id=0, has_side_effects=True, vmem_limit_bytes=54 * 1024 * 1024
        ),
    )(hidden, head_weight, teacher_logits)
    div, hg, dw = pl.pallas_call(
        put,
        name="put",
        out_shape=(
            jax.ShapeDtypeStruct((BLK,), F32),
            jax.ShapeDtypeStruct((SUB, WID), BF16),
            jax.ShapeDtypeStruct((WID, COLS), BF16),
        ),
        in_specs=[pl.BlockSpec(memory_space=vmem)] * 3,
        out_specs=[pl.BlockSpec(memory_space=pl.ANY)] * 3,
        scratch_shapes=[dma((6,))],
        compiler_params=pltpu.CompilerParams(vmem_limit_bytes=2 * 1024 * 1024),
    )(div, hg, dw)
    return div, hg, dw


def solution(mesh):
    return jax.shard_map(
        local,
        mesh=mesh,
        in_specs=(P("dp", None), P("dp", "vocab"), P("dp", "vocab")),
        out_specs=(P("dp"), P("vocab", "dp"), P("dp", "vocab")),
        check_vma=False,
    )
```

```python
import jax
import jax.numpy as jnp
from jax import lax
from jax.experimental import pallas as pl
from jax.experimental.pallas import tpu as pltpu
from jax.sharding import PartitionSpec as P

MESH = pl.DeviceIdType.MESH
F32, BF16 = jnp.float32, jnp.bfloat16
loss_scale = 256.0
LOW = -3.0e38

D, ROWS = 3584, 1024
NX, NY, NZ = 4, 4, 8
BLK = 128
SUB = BLK // NY
WID = D // 8
CHIP = 2 * WID
COLS = 4096
PART = COLS // NX
HSH = D // NY
THIN = BLK // NZ


STEPS = tuple((turn, first, 16) for turn, first in zip((3, 2, 3, 1, 2, 0, 1, 0), (0, 0, 16, 0, 16, 0, 16, 16)))
BEFORE = (None, 0, None, 1, 2, 3, 4, 6)
LAST = (5, 7)
FIRST = tuple(128 * s for s in range(8))
OFFERS = {0: 2, 1: 3, 2: 4, 3: 5, 4: 6, 6: 7}
EARLY = 112
WIDE = 512


def groups(value):
    return [value[:, 128 * g : 128 * g + 128] for g in range(value.shape[1] // 128)]


def fold(parts, op):
    while len(parts) > 1:
        parts = [op(parts[i], parts[i + 1]) for i in range(0, len(parts), 2)]
    return parts[0]


def row_max(part):
    return jnp.max(part.T, axis=0, keepdims=True)


def row_sum(part):
    return jnp.sum(part.T, axis=0, keepdims=True)


def kernel(
    h_ref, w_ref, t_ref,
    div_ref, hg_ref, dw_ref,
    hc, wc, tc, student, town, wown, wt, hx, ht, gbuf, acc,
    hgp, hgy, hgz, sx, sy, sz, last, col, cross, cx, cy, cz,
    lsem, own_s, own_r, two_s, two_r, wcs, wcr, ts, tr, hcs, hcr, sxs, sxr,
    gfs, gfr, hgys, hgyr, hgzs, hgzr, cxs, cxr, cys, cyr, czs, czr,
):
    dp, v = lax.axis_index("dp"), lax.axis_index("vocab")
    x, c = dp // 2, dp % 2
    z, y = v // NY, v % NY

    def at_x(o):
        return (lax.rem(x + o, NX) * 2 + c, v)

    def at_y(o):
        return (dp, z * NY + lax.rem(y + o, NY))

    def at_z(o):
        return (dp, lax.rem(z + o, NZ) * NY + y)

    other = (x * 2 + 1 - c, v)

    def remote(src, dst, ss, rs, device):
        return pltpu.make_async_remote_copy(
            src_ref=src, dst_ref=dst, send_sem=ss, recv_sem=rs, device_id=device, device_id_type=MESH
        )

    barrier = pltpu.get_barrier_semaphore()
    partners = [at_x(o) for o in range(1, NX)] + [other]
    partners += [at_y(o) for o in range(1, NY)] + [at_z(o) for o in range(1, NZ)]
    for p in partners:
        pl.semaphore_signal(barrier, inc=1, device_id=p, device_id_type=MESH)

    def cols_of(i):
        return pl.ds(pl.multiple_of(i * PART, PART), PART)

    def wrows(i, j):
        return pl.ds(pl.multiple_of(i * CHIP + j * WID, 64), WID)

    own_w = pltpu.make_async_copy(w_ref.at[:, cols_of(x)], wc.at[wrows(x, c)], lsem.at[0])
    share = pl.ds(pl.multiple_of(y * HSH, HSH), HSH)
    thin = [pl.ds(pl.multiple_of(lax.rem(z + NZ - o, NZ) * THIN, THIN), THIN) for o in range(NZ)]
    own_h = pltpu.make_async_copy(h_ref.at[thin[0], share], hc.at[x, thin[0], share], lsem.at[1])
    own_t = pltpu.make_async_copy(t_ref.at[:, cols_of(x)], tc.at[x], lsem.at[2])
    all_t = pltpu.make_async_copy(t_ref, town, lsem.at[3])
    all_w = pltpu.make_async_copy(w_ref, wown.at[pl.ds(0, WID)], lsem.at[4])
    for cp in (own_h, all_t, all_w, own_w, own_t):
        cp.start()
    pl.semaphore_wait(barrier, len(partners))

    h_x = [
        remote(
            h_ref.at[thin[0], share], hc.at[x, thin[0], share], own_s.at[o - 1], own_r.at[o - 1], at_x(o)
        )
        for o in range(1, NX)
    ]
    w_x = [
        remote(
            w_ref.at[:, cols_of(lax.rem(x + o, NX))], wc.at[wrows(x, c)], own_s.at[o + 2], own_r.at[o + 2], at_x(o)
        )
        for o in range(1, NX)
    ]
    t_x = [
        [
            remote(
                t_ref.at[rows, cols_of(lax.rem(x + o, NX))], tc.at[x, rows], ts.at[i, o - 1], tr.at[i, o - 1], at_x(o)
            )
            for o in range(1, NX)
        ]
        for i, rows in enumerate((pl.ds(0, EARLY), pl.ds(EARLY, BLK - EARLY)))
    ]

    def w_core(o):
        rows = wrows(lax.rem(x + NX - o, NX), c)
        src = w_ref.at[:, cols_of(x)] if o == 0 else wc.at[rows]
        return remote(src, wc.at[rows], wcs.at[o], wcr.at[o], other)

    w_c = [w_core(o) for o in range(NX)]
    for cp in h_x + w_x:
        cp.start()
    w_c[0].start()

    own_h.wait()
    for cp in h_x:
        cp.wait_recv()
    shares = [hc.at[:, rows, share] for rows in thin]
    h_z = [remote(shares[0], shares[0], two_s.at[o - 1, 3], two_r.at[o - 1, 3], at_z(o)) for o in range(1, NZ)]
    h_y = [
        [remote(part, part, two_s.at[i, o - 1], two_r.at[i, o - 1], at_y(o)) for o in range(1, NY)]
        for i, part in enumerate(shares)
    ]
    nearest = (1, 7, 2, 6, 3, 5, 4)
    for cp in [h_z[o - 1] for o in nearest] + h_y[0]:
        cp.start()

    for b in range(NX):
        sy[y, b] = jnp.where(lax.broadcasted_iota(jnp.int32, (8, BLK), 0) % 2 == 0, LOW, 0.0)
    all_t.wait()
    part = fold([town[:, 128 * g : 128 * g + 128] for g in range(COLS // 128)], jnp.maximum)
    top = jnp.max(part, axis=1, keepdims=True)
    total = fold([jnp.exp(town[:, 128 * g : 128 * g + 128] - top) for g in range(COLS // 128)], jnp.add)
    sy[y, x, 2:3, :] = row_max(part)
    sy[y, x, 3:4, :] = row_sum(total)

    all_w.wait()
    wown[WID:] = jnp.zeros((WIDE - WID, COLS), BF16)

    def turn(i, carry):
        cols = pl.ds(pl.multiple_of(i * 512, 512), 512)
        wt[cols, :] = wown[:, cols].T
        return carry

    lax.fori_loop(0, COLS // 512, turn, 0)

    for o in nearest:
        h_z[o - 1].wait_recv()
        for cp in h_y[o]:
            cp.start()
    for o in (1, 3, 2):
        w_x[o - 1].wait_recv()
        w_c[o].start()
    for cp in t_x[0]:
        cp.start()
    for cp in sum(h_y, []):
        cp.wait_recv()

    mine = pl.ds(pl.multiple_of(x * CHIP, CHIP), CHIP)
    h_c = remote(hc.at[:, :, mine], hx.at[c], hcs.at[0], hcr.at[0], other)
    h_c.start()
    keep = pltpu.make_async_copy(hc.at[:, :, mine], hx.at[c], lsem.at[5])
    keep.start()
    own_w.wait()
    for cp in w_c:
        cp.wait_recv()

    def score(i, carry):
        cols = pl.ds(pl.multiple_of(i * 256, 256), 256)
        tile = jnp.dot(hc[...].reshape(NX * BLK, D), wc[:, cols], preferred_element_type=F32)
        student[:, :, cols] = tile.reshape(NX, BLK, 256)
        return carry

    lax.fori_loop(0, PART // 256, score, 0)

    def local_stats(b, carry):
        parts = groups(student[b])
        part = fold(parts, jnp.maximum)
        top = jnp.max(part, axis=1, keepdims=True)
        total = fold([jnp.exp(p - top) for p in parts], jnp.add)
        sy[y, b, 0:1, :] = row_max(part)
        sy[y, b, 1:2, :] = row_sum(total)
        return carry

    lax.fori_loop(0, NX, local_stats, 0)

    def reduce_stats(slots, count, target):
        for b in range(NX):
            m_s = fold([slots[i, b, 0:1, :] for i in range(count)], jnp.maximum)
            m_t = fold([slots[i, b, 2:3, :] for i in range(count)], jnp.maximum)
            l_s = fold([slots[i, b, 1:2, :] * jnp.exp(slots[i, b, 0:1, :] - m_s) for i in range(count)], jnp.add)
            l_t = fold([slots[i, b, 3:4, :] * jnp.exp(slots[i, b, 2:3, :] - m_t) for i in range(count)], jnp.add)
            target(b, m_s, l_s, m_t, l_t)

    def into(slots, me):
        def put(b, *values):
            for r, value in enumerate(values):
                slots[me, b, r : r + 1, :] = value

        return put

    s_x = [remote(sx.at[x], sx.at[x], sxs.at[o - 1], sxr.at[o - 1], at_x(o)) for o in range(1, NX)]
    s_y = [remote(sy.at[y], sy.at[y], own_s.at[o + 5], own_r.at[o + 5], at_y(o)) for o in range(1, NY)]
    s_z = [remote(sz.at[z], sz.at[z], own_s.at[o + 8], own_r.at[o + 8], at_z(o)) for o in range(1, NZ)]
    for cp in s_y:
        cp.start()
    for cp in s_y:
        cp.wait_recv()
    reduce_stats(sy, NY, into(sz, z))
    for cp in s_z:
        cp.start()
    for cp in s_z:
        cp.wait_recv()
    reduce_stats(sz, NZ, into(sx, x))
    for cp in s_x + t_x[1]:
        cp.start()
    for cp in s_x:
        cp.wait_recv()
    def columns(b, m_s, l_s, m_t, l_t):
        for r, value in enumerate((m_s, loss_scale / l_s, m_t, loss_scale / l_t)):
            col[r, b] = jnp.broadcast_to(value, (BLK, BLK)).T
        last[b, 0:1, :] = m_s + jnp.log(l_s) - m_t - jnp.log(l_t)
        last[b, 1:2, :] = l_t

    reduce_stats(sx, NX, columns)

    keep.wait()
    h_c.wait_recv()
    for cp in h_x + w_x + h_z + sum(h_y, []) + s_x + s_y + s_z:
        cp.wait_send()
    own_t.wait()
    for cp in t_x[0] + t_x[1]:
        cp.wait_recv()

    def rows_at(s, plane):
        turn = STEPS[s][0]
        k = lax.rem(y + turn, NY) if plane == 0 else lax.rem(y + NY - turn, NY)
        return pl.ds(pl.multiple_of(k * SUB + STEPS[s][1], 16), STEPS[s][2])

    def rows_mine(s):
        turn = STEPS[s][0]
        k = lax.rem(y + turn + c * (2 * NY - 2 * turn), NY)
        return pl.ds(pl.multiple_of(k * SUB + STEPS[s][1], 16), STEPS[s][2])

    def piece(s, owner, part, parts):
        size = NX * STEPS[s][2]
        first = FIRST[s] + c * size + part * (size // parts)
        return gbuf.at[pl.ds(pl.multiple_of(first, 32), size // parts), cols_of(owner)]

    left, right, far = lax.rem(x + 3, NX), lax.rem(x + 1, NX), lax.rem(x + 2, NX)
    owners = [x, left, far, right]
    g_a, g_f, g_c = [], [], []
    for s in range(len(STEPS)):
        own, low, high = piece(s, x, 0, 1), piece(s, left, 0, 2), piece(s, right, 1, 2)
        g_a.append([remote(own, own, own_s.at[2 * s + i], own_r.at[2 * s + i], at_x(o)) for i, o in enumerate((1, 3))])
        g_f.append(
            [
                remote(low, low, gfs.at[s, 0], gfr.at[s, 0], at_x(1)),
                remote(high, high, gfs.at[s, 1], gfr.at[s, 1], at_x(3)),
            ]
        )
        blocks = [piece(s, q, 0, 1) for q in owners]
        g_c.append([remote(q, q, two_s.at[s, o], two_r.at[s, o], other) for o, q in enumerate(blocks)])

    def make(s):
        rows, count = rows_mine(s), STEPS[s][2]

        def grad(b, carry):
            m_s, a_s, m_t, a_t = [col[r, b, rows, :] for r in range(4)]
            out = pl.ds(pl.multiple_of(FIRST[s] + c * (NX * count) + b * count, 16), count)
            total = jnp.zeros((count, 128), F32)
            tiles = []
            for g in range(PART // 128):
                st = student[b, rows, 128 * g : 128 * g + 128]
                te = tc[b, rows, 128 * g : 128 * g + 128]
                e_t = jnp.exp(te - m_t)
                total += e_t * (te - st)
                tiles.append((jnp.exp(st - m_s) * a_s - e_t * a_t).astype(BF16))
            gbuf[out, cols_of(x)] = jnp.concatenate(tiles, axis=1)
            cross[b, rows, :] = total
            return carry

        lax.fori_loop(0, NX, grad, 0)

    def offer(s):
        for cp in g_a[s]:
            cp.start()
        g_c[s][0].start()

    def pass_on(s):
        for i, o in enumerate((1, 3)):
            g_a[s][i].wait_recv()
            g_f[s][i].start()
            g_c[s][o].start()

    make(0)
    offer(0)
    for s in range(1, len(STEPS)):
        make(s)
    for b in range(NX):
        cx[x, b] = jnp.broadcast_to(row_sum(cross[b]), (8, BLK))
    offer(1)

    for s in range(len(STEPS)):
        count = STEPS[s][2]
        block = jnp.concatenate([hx[j, b, rows_at(s, j), :] for j in range(2) for b in range(NX)], axis=0)
        block = pltpu.roll(block.astype(F32), lax.rem(c * WID, CHIP), 1)[:, :512]
        ht[:, FIRST[s] : FIRST[s] + 2 * NX * count] = block.T[:WID].astype(BF16)

    c_x = [
        remote(
            cx.at[x, lax.rem(x + o, NX)], cx.at[x, lax.rem(x + o, NX)], cxs.at[o - 1], cxr.at[o - 1], at_x(o)
        )
        for o in range(1, NX)
    ]
    c_y = [remote(cy.at[y], cy.at[y], cys.at[o - 1], cyr.at[o - 1], at_y(o)) for o in range(1, NY)]
    c_z = [remote(cz.at[z], cz.at[z], czs.at[o - 1], czr.at[o - 1], at_z(o)) for o in range(1, NZ)]

    def to_y(s, j):
        rows = pl.ds(s * BLK + j * 64, 64)
        return remote(hgp.at[rows], hgy.at[rows], hgys.at[s, j], hgyr.at[s, j], at_y(NY - 1 if j else 1))

    def to_z(i, o):
        zz = lax.rem(z + o, NZ)
        rows = pl.ds(pl.multiple_of(LAST[i] * BLK + (zz % 2) * 64 + (zz // 2) * 16, 16), 16)
        return remote(hgp.at[rows], hgz.at[o - 1, pl.ds(16 * i, 16)], hgzs.at[i, o - 1], hgzr.at[i, o - 1], at_z(o))

    h_to_y = [[to_y(s, j) for j in range(2)] if STEPS[s][0] else [] for s in range(len(STEPS))]
    h_to_z = [[to_z(i, o) for o in range(1, NZ)] for i in range(2)]

    def far_in(s):
        for cp in g_f[s]:
            cp.wait_recv()
        g_c[s][2].start()

    def product(s):
        for cp in g_c[s]:
            cp.wait_recv()
        rows = slice(FIRST[s], FIRST[s] + BLK)
        hgp[rows] = jnp.dot(gbuf[rows], wt[...], preferred_element_type=F32)
        if BEFORE[s] is not None:
            for cp in h_to_y[BEFORE[s]]:
                cp.wait_recv()
            hgp[rows] += hgy[FIRST[BEFORE[s]] : FIRST[BEFORE[s]] + BLK]
        for cp in h_to_y[s] or h_to_z[LAST.index(s)]:
            cp.start()

    def head_product(i, first, last):
        depth = slice(512 * i, 512 * i + 512)

        def head(n, carry):
            cols = pl.ds(pl.multiple_of(n * 512, 512), 512)
            tile = jnp.dot(ht[:, depth], gbuf[depth, cols], preferred_element_type=F32)
            if i == 0:
                acc[:, cols] = tile
            else:
                dw_ref[:, cols] = (acc[:, cols] + tile).astype(BF16)
            return carry

        lax.fori_loop(first, last, head, 0)

    def near(s):
        pass_on(s)
        if s in OFFERS:
            offer(OFFERS[s])

    near(0)
    near(1)
    for cp in c_x:
        cp.start()
    near(2)
    far_in(0)
    product(0)
    far_in(1)
    near(3)
    far_in(2)
    product(1)
    for cp in c_x:
        cp.wait_recv()
    cy[y] = cx[0, x] + cx[1, x] + cx[2, x] + cx[3, x]
    for cp in c_y:
        cp.start()
    near(4)
    product(2)
    far_in(3)
    product(3)
    far_in(4)
    near(5)
    near(6)
    for cp in c_y:
        cp.wait_recv()
    cz[z] = cy[0] + cy[1] + cy[2] + cy[3]
    for cp in c_z:
        cp.start()
    product(4)
    far_in(5)
    product(5)
    far_in(6)
    near(7)
    product(6)
    far_in(7)
    product(7)
    head_product(0, 0, 8)
    head_product(1, 0, 8)

    for cp in c_z:
        cp.wait_recv()
    crossed = fold([cz[i, 0:1, :] for i in range(NZ)], jnp.add)
    div_ref[...] = (crossed / last[x, 1:2, :] + last[x, 0:1, :])[0]

    for i in range(2):
        for cp in h_to_z[i]:
            cp.wait_recv()
        mine = pl.ds(pl.multiple_of(LAST[i] * BLK + (z % 2) * 64 + (z // 2) * 16, 16), 16)
        total = hgp[mine, :]
        for o in range(NZ - 1):
            total = total + hgz[o, 16 * i : 16 * i + 16]
        hg_ref[16 * i : 16 * i + 16, :] = total[:, :WID].astype(BF16)

    sent = [h_c] + w_c + c_x + c_y + c_z
    for cp in sent + sum(t_x + g_a + g_f + g_c + h_to_y + h_to_z, []):
        cp.wait_send()


def put(div_in, hg_in, dw_in, div_ref, hg_ref, dw_ref, sems):
    rows = WID // 4
    parts = [(dw_in.at[pl.ds(rows * i, rows)], dw_ref.at[pl.ds(rows * i, rows)]) for i in range(4)]
    parts += [(div_in, div_ref), (hg_in, hg_ref)]
    copies = [pltpu.make_async_copy(src, dst, sems.at[i]) for i, (src, dst) in enumerate(parts)]
    for cp in copies:
        cp.start()
    for cp in copies:
        cp.wait()


def local(hidden, head_weight, teacher_logits):
    dma = pltpu.SemaphoreType.DMA
    vmem = pltpu.VMEM
    scratch = [
        vmem((NX, BLK, D), BF16),
        vmem((D, PART), BF16),
        vmem((NX, BLK, PART), F32),
        vmem((NX, BLK, PART), F32),
        vmem((BLK, COLS), F32),
        vmem((WIDE, COLS), BF16),
        vmem((COLS, WIDE), BF16),
        vmem((2, NX, BLK, CHIP), BF16),
        vmem((WID, ROWS), BF16),
        vmem((ROWS, COLS), BF16),
        vmem((WID, COLS), F32),
        vmem((ROWS, WIDE), F32),
        vmem((ROWS, WIDE), F32),
        vmem((NZ - 1, SUB, WIDE), F32),
        vmem((NX, NX, 8, BLK), F32),
        vmem((NY, NX, 8, BLK), F32),
        vmem((NZ, NX, 8, BLK), F32),
        vmem((NX, 8, BLK), F32),
        vmem((4, NX, BLK, BLK), F32),
        vmem((NX, BLK, BLK), F32),
        vmem((NX, NX, 8, BLK), F32),
        vmem((NY, 8, BLK), F32),
        vmem((NZ, 8, BLK), F32),
    ]
    counts = [(16,), (8, 4), (4,), (2, 3), (1,), (3,), (8, 2), (8, 2), (2, 7), (3,), (3,), (7,)]
    sems = [dma((6,))]
    for n in counts:
        sems += [dma(n), dma(n)]
    div, hg, dw = pl.pallas_call(
        kernel,
        name="distill",
        out_shape=(vmem((BLK,), F32), vmem((SUB, WID), BF16), vmem((WID, COLS), BF16)),
        in_specs=[pl.BlockSpec(memory_space=pl.ANY)] * 3,
        out_specs=[pl.BlockSpec(memory_space=vmem)] * 3,
        scratch_shapes=scratch + sems,
        compiler_params=pltpu.CompilerParams(
            collective_id=0, has_side_effects=True, vmem_limit_bytes=54 * 1024 * 1024
        ),
    )(hidden, head_weight, teacher_logits)
    div, hg, dw = pl.pallas_call(
        put,
        name="put",
        out_shape=(
            jax.ShapeDtypeStruct((BLK,), F32),
            jax.ShapeDtypeStruct((SUB, WID), BF16),
            jax.ShapeDtypeStruct((WID, COLS), BF16),
        ),
        in_specs=[pl.BlockSpec(memory_space=vmem)] * 3,
        out_specs=[pl.BlockSpec(memory_space=pl.ANY)] * 3,
        scratch_shapes=[dma((6,))],
        compiler_params=pltpu.CompilerParams(vmem_limit_bytes=2 * 1024 * 1024),
    )(div, hg, dw)
    return div, hg, dw


def solution(mesh):
    return jax.shard_map(
        local,
        mesh=mesh,
        in_specs=(P("dp", None), P("dp", "vocab"), P("dp", "vocab")),
        out_specs=(P("dp"), P("vocab", "dp"), P("dp", "vocab")),
        check_vma=False,
    )
```
